32 devices in a mesh: ckpt: 4 (over z), tok: 4 (over x, core), vocab: 2 (over y).
Axes of the slice: x: 2, y: 2, z: 4, core: 2. Of those that a mesh axis runs over, the one named last changes fastest.
Arguments:
- heads: bfloat16 [4, 2560, 10240], P('ckpt', 'tok', 'vocab'), may hold values from -5 to 5
- hidden: bfloat16 [4, 512, 2560], P('ckpt', 'tok'), may hold values from -4 to 4
- targets: int32 [512], P('tok'), may hold values from 0 to 10239
Outputs:
- merged: bfloat16 [2560, 10240], P(('ckpt', 'tok'), 'vocab')
The draws below stay inside these ranges and needn't reach their ends.
All inputs are finite; a program needn't handle non-finite values.
Results may differ from the reference program's by a relative error of at most 0.0044.
Values may be sent and summed in bfloat16 or wider, within the bound.
No kernel may reach another device: no remote copies, remote signals or barrier semaphores. Data moves between devices by JAX's collectives and lax.ppermute only.
A program may use at most 128 MiB of HBM per device.

```python
import math
import jax
import jax.numpy as jnp
from jax import lax

D = 2560
TOKENS = 512
VOCAB = 10240
CKPTS = 4


def head_column(key, check, index):
    column = jax.random.normal(jax.random.fold_in(jax.random.fold_in(key, check), index), (D,), jnp.float32)
    return jnp.clip(column, -5.0, 5.0)


def draw_heads(key, part):
    layers = []
    for check in range(CKPTS):
        columns = jax.vmap(lambda index: head_column(key, check, index))(jnp.arange(VOCAB))
        layers.append(jnp.transpose(columns).astype(jnp.bfloat16))
    return jnp.stack(layers)


def draw_hidden(key, part):
    own = jax.random.fold_in(key, 7)
    keys = jax.random.split(own, 3)
    shape = (CKPTS, TOKENS, D)
    token_scale = jnp.exp(jax.random.uniform(keys[1], (CKPTS, TOKENS, 1), jnp.float32, -1.15, 1.15))
    feature_scale = jnp.exp(jax.random.uniform(keys[2], (CKPTS, 1, D), jnp.float32, -1.15, 1.15))
    base = jnp.clip(jax.random.normal(keys[0], shape, jnp.float32), -4.0, 4.0)
    values = base * token_scale * feature_scale * float(D) ** (-0.5)
    return jnp.clip(values, -4.0, 4.0).astype(jnp.bfloat16)


def touch_ends(drawn, stream_key, low, high):
    longest = drawn.shape.index(max(drawn.shape))
    spots = []
    for shift in (0, 1):
        where = [jax.random.randint(jax.random.fold_in(stream_key, axis), (), 0, length) for axis, length in enumerate(drawn.shape)]
        where[longest] = (where[longest] + shift) % drawn.shape[longest]
        spots.append(tuple(where))
    return drawn.at[spots[0]].set(low).at[spots[1]].set(high)


def setup_inputs(seed: int = 0) -> dict:
    key_of = jax.random.split(jax.random.key(seed), 4)
    return {
        "heads": draw_heads(jax.random.fold_in(key_of[3], 71), 0),
        "hidden": draw_hidden(jax.random.fold_in(key_of[3], 71), 0),
        "targets": touch_ends(jax.random.randint(key_of[2], (TOKENS,), 0, VOCAB), jax.random.fold_in(key_of[2], 1), 0, VOCAB - 1).astype(jnp.int32),
    }


prior_weight = 0.05


def reference(heads, hidden, targets):
    hidden_sq = jnp.square(hidden.astype(jnp.float32)).astype(jnp.bfloat16)
    column_ids = jnp.arange(VOCAB, dtype=jnp.int32)
    resid_list = []
    level_list = []
    for check in range(CKPTS):
        logits = jnp.dot(hidden[check], heads[check], preferred_element_type=jnp.float32)
        top = jnp.max(logits, axis=1, keepdims=True)
        shifted = jnp.exp(logits - top)
        total = jnp.sum(shifted, axis=1, keepdims=True)
        onehot = (targets[:, None] == column_ids[None, :]).astype(jnp.float32)
        resid_sq = jnp.square(shifted / total - onehot).astype(jnp.bfloat16)
        row_h = jnp.sum(hidden_sq[check].astype(jnp.float32), axis=1)
        row_r = jnp.sum(resid_sq.astype(jnp.float32), axis=1)
        level = jnp.sum(row_h * row_r) / jnp.float32(TOKENS * D * VOCAB)
        resid_list.append(resid_sq)
        level_list.append(level)
    resid_all = jnp.stack(resid_list)
    levels = jnp.stack(level_list)
    block = math.gcd(VOCAB, 2048)
    starts = jnp.arange(VOCAB // block, dtype=jnp.int32) * block

    def one_block(start):
        numer = jnp.zeros((D, block), jnp.float32)
        denom = jnp.zeros((D, block), jnp.float32)
        for check in range(CKPTS):
            piece = lax.dynamic_slice_in_dim(resid_all[check], start, block, 1)
            fisher = lax.dot_general(hidden_sq[check], piece, (((0,), (0,)), ((), ())),
                                     preferred_element_type=jnp.float32) / jnp.float32(TOKENS)
            weight = (jnp.float32(VOCAB) * fisher / levels[check] + prior_weight).astype(jnp.bfloat16)
            weight_wide = weight.astype(jnp.float32)
            head_block = lax.dynamic_slice_in_dim(heads[check], start, block, 1)
            numer = numer + weight_wide * head_block.astype(jnp.float32)
            denom = denom + weight_wide
        return (numer / denom).astype(jnp.bfloat16)

    blocks = lax.map(one_block, starts)
    return jnp.transpose(blocks, (1, 0, 2)).reshape(D, VOCAB)
```

```python
import functools

import jax
import jax.numpy as jnp
from jax import lax
from jax.experimental import pallas as pl
from jax.experimental.pallas import tpu as pltpu
from jax.sharding import PartitionSpec as P

prior_weight = 0.05
VMEM = 56 * 1024 * 1024


def score_kernel(turn_ref, *refs):
    states, blocks, out_ref = refs[0:4], refs[4:8], refs[8]
    total = None
    for far in range(4):
        dot = jnp.dot(states[far][...], blocks[far][...], preferred_element_type=jnp.float32)
        total = dot if total is None else total + dot
    out_ref[...] = total


def score(turns, states, blocks):
    tokens = states.shape[0]
    depth, width = blocks[0].shape
    tile = 256 if width % 256 == 0 else 128

    def part(far):
        return pl.BlockSpec((tokens, depth), lambda i, s: (0, s[far]))

    return pl.pallas_call(
        score_kernel,
        out_shape=jax.ShapeDtypeStruct((tokens, width), jnp.float32),
        grid_spec=pltpu.PrefetchScalarGridSpec(
            num_scalar_prefetch=1,
            grid=(width // tile,),
            in_specs=[part(far) for far in range(4)]
            + [pl.BlockSpec((depth, tile), lambda i, s: (0, i))] * 4,
            out_specs=pl.BlockSpec((tokens, tile), lambda i, s: (0, i)),
        ),
        compiler_params=pltpu.CompilerParams(vmem_limit_bytes=VMEM),
        cost_estimate=pl.CostEstimate(flops=0, bytes_accessed=0, transcendentals=0),
        name="score",
    )(turns, *([states] * 4), *blocks)


def merge_kernel(scale_ref, *refs):
    heads, resids, hiddens, out_ref = refs[0:4], refs[4:8], refs[8:12], refs[12]
    numer = denom = None
    for slot in range(4):
        product = lax.dot_general(
            hiddens[slot][...], resids[slot][...], (((1,), (0,)), ((), ())),
            preferred_element_type=jnp.float32,
        )
        scaled = (product * scale_ref[4]) * scale_ref[slot]
        weight = (scaled + prior_weight).astype(jnp.bfloat16).astype(jnp.float32)
        term = weight * heads[slot][...].astype(jnp.float32)
        numer = term if numer is None else numer + term
        denom = weight if denom is None else denom + weight
    out_ref[...] = (numer / denom).astype(out_ref.dtype)


def merge(scales, heads, resids, hiddens, start):
    rows, width = heads[0].shape
    tokens = resids[0].shape[0]
    tile = rows // 2
    tall = pl.BlockSpec((tile, width), lambda i: (i, 0))
    resid = pl.BlockSpec((tokens, width), lambda i: (0, 0))
    hidden = pl.BlockSpec((tile, tokens), lambda i: (i, 0))
    return pl.pallas_call(
        merge_kernel,
        out_shape=jax.ShapeDtypeStruct((rows, width), jnp.bfloat16),
        grid=(rows // tile,),
        in_specs=[pl.BlockSpec(memory_space=pltpu.SMEM)] + [tall] * 4 + [resid] * 4 + [hidden] * 4,
        out_specs=tall,
        compiler_params=pltpu.CompilerParams(vmem_limit_bytes=VMEM),
        cost_estimate=pl.CostEstimate(flops=0, bytes_accessed=0, transcendentals=0),
        name="merge",
    )(scales, *heads, *[x[:, start : start + width] for x in resids], *hiddens)


def after(value, *earlier):
    return lax.optimization_barrier((value, *earlier))[0] if earlier else value


def shards(heads, hidden, targets):
    ntok = lax.axis_size("tok")
    nckpt = lax.axis_size("ckpt")
    nvocab = lax.axis_size("vocab")
    assert ntok == nckpt == 4
    tok = lax.axis_index("tok")
    ckpt = lax.axis_index("ckpt")
    rows = heads[0]
    depth = rows.shape[0]
    width = rows.shape[1] // ntok
    per_device, features_all = hidden.shape[1:]
    tokens = per_device * ntok
    part = width // 5

    def swap(x, far):
        return lax.ppermute(x, "tok", [(t, t ^ far) for t in range(ntok)])

    def from_plane(x, far):
        return lax.ppermute(x, "ckpt", [(c, (c - far) % nckpt) for c in range(nckpt)])

    def shift(x, step, first):
        pairs = [(c, c + step) for c in range(nckpt) if 0 <= c + step < nckpt]
        return lax.ppermute(x, "ckpt", pairs[first:] if step > 0 else pairs[: len(pairs) - first])

    def columns_of(far, lo, w):
        return lax.dynamic_slice(rows, (0, (tok ^ far) * width + lo), (depth, w))

    own, beside = columns_of(0, 0, width), swap(columns_of(1, 0, width), 1)

    def cross(lo, w, deps, extra=None):
        two, three = columns_of(2, lo, w), columns_of(3, lo, w)
        if extra is not None:
            two = jnp.concatenate([two, extra], axis=1)
        return swap(after(two, *deps), 2), swap(after(three, *deps), 3)

    def spread(two, three, lo, skip, w, deps, extra=None):
        def pick(plane):
            return lax.select_n(
                tok ^ plane, own[:, lo : lo + w], beside[:, lo : lo + w],
                two[:, skip : skip + w], three[:, skip : skip + w],
            )

        out = [pick(ckpt)]
        for far in (1, 2, 3):
            plane = (ckpt - far) % nckpt
            piece = pick(plane)
            if extra is not None:
                piece = jnp.concatenate([piece, extra(plane).reshape(-1, w)])
            out.append(from_plane(after(piece, *deps), far))
        return out

    def by_tok(x):
        return jnp.stack([lax.dynamic_index_in_dim(x, tok ^ t, 0, keepdims=False) for t in range(4)])

    two_a, three_a = cross(0, part, ())
    first = (two_a, three_a, beside)

    def features_for(plane):
        return lax.dynamic_slice_in_dim(hidden[0], plane * depth, depth, 1)

    heads_a = spread(two_a, three_a, 0, 0, part, first, features_for)
    two_b, three_b = cross(part, 2 * part, first, hidden[0].reshape(depth, -1))
    second = (two_b, three_b, *heads_a[1:])

    heads_b = spread(two_b, three_b, part, 0, part, second)
    two_c, three_c = cross(3 * part, 2 * part, second)
    near = jnp.stack([hidden[0], two_b[:, 2 * part :].reshape(per_device, -1)])
    pairs = [[t, t + 1] for t in range(0, ntok, 2)]
    states = lax.all_gather(after(near, *second), "tok", axis=0, axis_index_groups=pairs)
    core = tok % 2
    states = jnp.stack(
        [lax.dynamic_index_in_dim(states[:, chip], core ^ c, 0, keepdims=False) for chip in (0, 1) for c in (0, 1)]
    )
    states = by_tok(states).reshape(tokens, features_all)
    third = (two_c, three_c, *heads_b[1:])

    heads_c = spread(two_b, three_b, 2 * part, part, part, third)
    fourth = tuple(heads_c[1:])
    packed = jnp.stack(
        [features_for(ckpt)] + [x[depth:].reshape(per_device, depth) for x in heads_a[1:]]
    )
    features = lax.all_gather(after(packed, *third), "tok", axis=1, tiled=True)
    heads_a = heads_a[:1] + [x[:depth] for x in heads_a[1:]]

    turns = jnp.stack([tok ^ far for far in range(4)]).astype(jnp.int32)
    pieces = [
        score(turns, states, [own[:, lo : lo + w], beside[:, lo : lo + w], two[:, :w], three[:, :w]])
        for lo, w, two, three in (
            (0, part, two_a, three_a), (part, 2 * part, two_b, three_b), (3 * part, 2 * part, two_c, three_c)
        )
    ]
    peak = functools.reduce(jnp.maximum, [jnp.max(x, axis=1) for x in pieces])
    mass = sum(jnp.sum(jnp.exp(x - peak[:, None]), axis=1) for x in pieces)
    local = jnp.concatenate([peak, mass, targets.astype(jnp.float32)])
    every = lax.all_gather(after(local, *third), ("tok", "vocab"), axis=0)
    both = every[:, : 2 * tokens].reshape(-1, 2, tokens)
    top = jnp.max(both[:, 0], axis=0)
    total = jnp.sum(both[:, 1] * jnp.exp(both[:, 0] - top[None]), axis=0)
    labels = every[:, 2 * tokens :].reshape(ntok, nvocab, -1)[:, 0].reshape(-1).astype(jnp.int32)

    offset = (lax.axis_index("vocab") * ntok + tok) * width
    resids = []
    for x, lo in zip(pieces, (0, part, 3 * part)):
        ids = offset + lo + jnp.arange(x.shape[1], dtype=jnp.int32)
        onehot = (labels[:, None] == ids[None, :]).astype(jnp.float32)
        shifted = jnp.exp(x - top[:, None]) / total[:, None]
        resids.append(jnp.square(shifted - onehot).astype(jnp.bfloat16))
    resid_sq = jnp.concatenate(resids, axis=1)

    up = [resid_sq, shift(after(resid_sq, *fourth), 1, 0)]
    down = [resid_sq, shift(after(resid_sq, *fourth), -1, 0)]
    fifth = (up[1], down[1])
    up.append(shift(after(up[1], *fifth), 1, 1))
    down.append(shift(after(down[1], *fifth), -1, 1))
    up.append(lax.ppermute(after(up[1], *fifth), "ckpt", [(1, 3)]))
    down.append(lax.ppermute(after(down[1], *fifth), "ckpt", [(2, 0)]))
    sixth = (up[2], down[2], up[3], down[3])
    heads_d = spread(two_c, three_c, 3 * part, 0, 2 * part, sixth)

    vocab_total = width * ntok * nvocab
    hidden_rows = jnp.sum(
        jnp.square(states.astype(jnp.float32)).astype(jnp.bfloat16).astype(jnp.float32), axis=1
    )
    share = jnp.sum(hidden_rows * jnp.sum(resid_sq.astype(jnp.float32), axis=1))
    count = float(tokens * features_all * vocab_total)
    level = lax.psum(share, ("tok", "vocab")) / jnp.float32(count)
    inverse = jnp.full((8, 128), 1.0 / level, jnp.float32)
    inverses = [inverse] + [from_plane(after(inverse, *fifth), far) for far in (1, 2, 3)]
    scales = jnp.stack(
        [x[0, 0] for x in inverses] + [jnp.float32(vocab_total / tokens)]
    )

    resid_of = [resid_sq]
    for far in range(1, nckpt):
        resid_of.append(jnp.where(ckpt + far < nckpt, down[far], up[nckpt - far]))

    features_sq = [
        jnp.square(features[far].astype(jnp.float32)).astype(jnp.bfloat16).T
        for far in range(nckpt)
    ]

    own_rows = depth // ntok
    result = jnp.zeros((own_rows, width * ntok), jnp.bfloat16)
    for block, lo in ((heads_a, 0), (heads_b, part), (heads_c, 2 * part), (heads_d, 3 * part)):
        blended = merge(scales, block, resid_of, features_sq, lo)
        for far in (2, 3, 1, 0):
            piece = lax.dynamic_slice_in_dim(blended, (tok ^ far) * own_rows, own_rows, 0)
            if far:
                piece = swap(piece, far)
            result = lax.dynamic_update_slice(result, piece, (0, (tok ^ far) * width + lo))
    return result


def solution(mesh):
    placed = (P("ckpt", "tok", "vocab"), P("ckpt", "tok", None), P("tok"))
    return jax.shard_map(
        shards, mesh=mesh, in_specs=placed, out_specs=P(("ckpt", "tok"), "vocab"), check_vma=False
    )
```

```python
import jax
import jax.numpy as jnp
from jax import lax
from jax.experimental import pallas as pl
from jax.experimental.pallas import tpu as pltpu
from jax.sharding import PartitionSpec as P

prior_weight = 0.05
VMEM = 56 * 1024 * 1024
BOTH = ("ckpt", "tok")


def call(kernel, name, **options):
    return pl.pallas_call(
        kernel, name=name, compiler_params=pltpu.CompilerParams(vmem_limit_bytes=VMEM), **options
    )


def pack_kernel(*refs):
    parts, (wide_ref, narrow_ref) = refs[:-2], refs[-2:]
    peers, _, _, wide = wide_ref.shape
    narrow = narrow_ref.shape[2] // len(parts)
    split = peers * wide
    for g in range(peers):
        for q, part in enumerate(parts):
            wide_ref[g, q] = part[:, g * wide : (g + 1) * wide]
        lo = split + g * narrow
        narrow_ref[g] = jnp.concatenate([part[:, lo : lo + narrow] for part in parts], axis=1)


def pack(rows, peers, wide, narrow, fold):
    depth, columns = rows.shape
    height = depth // fold
    tall = 32
    steps = height // tall

    def part(q):
        return pl.BlockSpec((tall, columns), lambda i: (q * steps + i, 0))

    wide_out, narrow_out = call(
        pack_kernel, "pack",
        out_shape=(
            jax.ShapeDtypeStruct((peers, fold, height, wide), rows.dtype),
            jax.ShapeDtypeStruct((peers, height, fold * narrow), rows.dtype),
        ),
        grid=(steps,),
        in_specs=[part(q) for q in range(fold)],
        out_specs=(
            pl.BlockSpec((peers, fold, tall, wide), lambda i: (0, 0, i, 0)),
            pl.BlockSpec((peers, tall, fold * narrow), lambda i: (0, i, 0)),
        ),
    )(*([rows] * fold))
    return wide_out.reshape(peers, depth, wide), narrow_out


def copy_kernel(in_ref, out_ref):
    out_ref[...] = in_ref[...]


def staged(x):
    block = pl.BlockSpec((1, *x.shape[1:]), lambda i: (i, 0, 0))
    return call(
        copy_kernel, "staged",
        out_shape=jax.ShapeDtypeStruct(x.shape, x.dtype),
        grid=(x.shape[0],),
        in_specs=[block],
        out_specs=block,
        cost_estimate=pl.CostEstimate(flops=5 * 10**10, bytes_accessed=2 * x.size * 2, transcendentals=0),
    )(x)


def square_kernel(states_ref, *refs):
    out_ref, sum_ref = refs[-2:]
    x = states_ref[...].reshape(-1, states_ref.shape[3]).astype(jnp.float32)
    turned = jnp.square(x).astype(jnp.bfloat16).T
    out_ref[0] = turned
    sum_ref[0] = jnp.sum(turned.astype(jnp.float32), axis=0, keepdims=True)


def squares(states, so_far, step, steps):
    groups, ckpts, size, features = states.shape
    tokens = groups * size
    tile = features // steps
    return call(
        square_kernel, "squares",
        out_shape=(
            jax.ShapeDtypeStruct((ckpts, features, tokens), jnp.bfloat16),
            jax.ShapeDtypeStruct((ckpts, 1, tokens), jnp.float32),
        ),
        grid=(ckpts,),
        in_specs=[pl.BlockSpec((groups, 1, size, tile), lambda c: (0, c, 0, step))]
        + [pl.BlockSpec(memory_space=pl.ANY)] * len(so_far),
        out_specs=(
            pl.BlockSpec((1, tile, tokens), lambda c: (c, step, 0)),
            pl.BlockSpec((1, 1, tokens), lambda c: (c, 0, 0)),
        ),
        input_output_aliases={1: 0} if so_far else {},
    )(states, *so_far)


def unfolded(block, fold):
    w = block.shape[1] // fold
    return jnp.concatenate([block[:, q * w : (q + 1) * w] for q in range(fold)], axis=0)


def score_kernel(states_ref, wide_ref, narrow_ref, labels_ref, ids_ref, wide_out, narrow_out, stats_ref):
    states = states_ref[...].reshape(-1, states_ref.shape[3])
    blocks, height, folded = narrow_ref.shape[1:]
    narrow = narrow_out.shape[2]
    heads = jnp.concatenate([unfolded(narrow_ref[0, b], folded // narrow) for b in range(blocks)], axis=0)
    parts = (
        jnp.dot(states, wide_ref[0], preferred_element_type=jnp.float32),
        jnp.dot(states, heads, preferred_element_type=jnp.float32),
    )
    wide_out[0], narrow_out[0] = parts
    wide = wide_out.shape[2]
    top = jnp.maximum(*[jnp.max(x, axis=1, keepdims=True) for x in parts])
    mass = square = hit = 0.0
    for x, columns in zip(parts, (ids_ref[:, :wide], ids_ref[:, wide:])):
        grown = jnp.exp(x - top)
        target = labels_ref[...] == columns
        mass += jnp.sum(grown, axis=1, keepdims=True)
        hit += jnp.sum(jnp.where(target, grown, 0.0), axis=1, keepdims=True)
        square += jnp.sum(jnp.where(target, 0.0, grown * grown), axis=1, keepdims=True)
    lane = lax.broadcasted_iota(jnp.int32, (top.shape[0], 128), 1)
    table = jnp.where(lane == 0, top, jnp.where(lane == 1, mass, jnp.where(lane == 2, square, hit)))
    stats_ref[0] = table.T[:8]


def score(states, wide, narrow, narrow_width, labels, ids):
    groups, ckpts, size, features = states.shape
    tokens = groups * size
    return call(
        score_kernel, "score",
        out_shape=(
            jax.ShapeDtypeStruct((ckpts, tokens, wide.shape[2]), jnp.float32),
            jax.ShapeDtypeStruct((ckpts, tokens, narrow_width), jnp.float32),
            jax.ShapeDtypeStruct((ckpts, 8, tokens), jnp.float32),
        ),
        grid=(ckpts,),
        in_specs=[
            pl.BlockSpec((groups, 1, size, features), lambda c: (0, c, 0, 0)),
            pl.BlockSpec((1, *wide.shape[1:]), lambda c: (c, 0, 0)),
            pl.BlockSpec((1, *narrow.shape[1:]), lambda c: (c, 0, 0, 0)),
            pl.BlockSpec(labels.shape, lambda c: (0, 0)),
            pl.BlockSpec(ids.shape, lambda c: (0, 0)),
        ],
        out_specs=(
            pl.BlockSpec((1, tokens, wide.shape[2]), lambda c: (c, 0, 0)),
            pl.BlockSpec((1, tokens, narrow_width), lambda c: (c, 0, 0)),
            pl.BlockSpec((1, 8, tokens), lambda c: (c, 0, 0)),
        ),
    )(states, wide, narrow, labels, ids)


def merge_kernel(
    scale_ref, wide_logits, narrow_logits, table_ref, labels_ref, ids_ref, hidden_ref, wide_ref, narrow_ref,
    out_ref, wide_resid, narrow_resid,
):
    ckpts, _, wide = wide_logits.shape
    narrow = narrow_logits.shape[2]
    fold = narrow_ref.shape[3] // narrow

    @pl.when(pl.program_id(0) == 0)
    def _():
        target = jnp.where(labels_ref[...] == ids_ref[...], 1.0, 0.0)
        for c in range(ckpts):
            top, total = table_ref[:, c : c + 1], table_ref[:, ckpts + c : ckpts + c + 1]
            for logits, resid, hot in (
                (wide_logits, wide_resid, target[:, :wide]), (narrow_logits, narrow_resid, target[:, wide:])
            ):
                share = jnp.exp(logits[c] - top) / total
                resid[c] = jnp.square(share - hot).astype(jnp.bfloat16)

    def blend(resid, heads_of):
        numer = denom = None
        for c in range(ckpts):
            product = jnp.dot(hidden_ref[c], resid[c], preferred_element_type=jnp.float32)
            scaled = (product * scale_ref[ckpts]) * scale_ref[c]
            weight = (scaled + prior_weight).astype(jnp.bfloat16).astype(jnp.float32)
            term = weight * heads_of(c).astype(jnp.float32)
            numer = term if numer is None else numer + term
            denom = weight if denom is None else denom + weight
        return numer / denom

    peers, own = out_ref.shape[0], wide_ref.shape[2] // out_ref.shape[0]
    merged = blend(wide_resid, lambda c: wide_ref[c, 0])
    out_ref[:, :own] = merged.astype(out_ref.dtype).reshape(peers, own, wide)
    merged = blend(narrow_resid, lambda c: unfolded(narrow_ref[c, 0], fold))
    height = own // fold
    for peer in range(peers):
        pieces = [merged[peer * own + q * height : peer * own + (q + 1) * height] for q in range(fold)]
        block = jnp.concatenate(pieces, axis=1)
        rest = jnp.zeros((out_ref.shape[1] - own - height, block.shape[1]), jnp.float32)
        out_ref[peer, own:] = jnp.concatenate([block, rest], axis=0).astype(out_ref.dtype)


def merge(scales, wide_logits, narrow_logits, table, labels, ids, hidden_sq, wide, narrow, ntok):
    ckpts, blocks, depth, width = wide.shape
    tokens, slim = narrow_logits.shape[1:]
    own = depth // ntok
    tall = own + -(-own * slim // width // 16) * 16

    def whole(x):
        return pl.BlockSpec(x.shape, lambda i: (0,) * x.ndim)

    return call(
        merge_kernel, "merge",
        out_shape=jax.ShapeDtypeStruct((blocks * ntok, tall, width), jnp.bfloat16),
        grid=(blocks,),
        in_specs=[pl.BlockSpec(memory_space=pltpu.SMEM)]
        + [whole(x) for x in (wide_logits, narrow_logits, table, labels, ids)]
        + [
            pl.BlockSpec((ckpts, depth, tokens), lambda i: (0, i, 0)),
            pl.BlockSpec((ckpts, 1, depth, width), lambda i: (0, i, 0, 0)),
            pl.BlockSpec((ckpts, 1, *narrow.shape[2:]), lambda i: (0, i, 0, 0)),
        ],
        out_specs=pl.BlockSpec((ntok, tall, width), lambda i: (i, 0, 0)),
        scratch_shapes=[
            pltpu.VMEM((ckpts, tokens, width), jnp.bfloat16), pltpu.VMEM((ckpts, tokens, slim), jnp.bfloat16)
        ],
    )(scales, wide_logits, narrow_logits, table, labels, ids, hidden_sq, wide, narrow)


def after(value, *earlier):
    return lax.optimization_barrier((value, *earlier))[0] if earlier else value


def exchange(x):
    return lax.all_to_all(x, BOTH, 0, 0, tiled=True)


def combined(x, y):
    top = jnp.maximum(x[0], y[0])
    fx, fy = jnp.exp(x[0] - top), jnp.exp(y[0] - top)
    return jnp.stack(
        [top, x[1] * fx + y[1] * fy, x[2] * (fx * fx) + y[2] * (fy * fy), x[3] * fx + y[3] * fy]
    )


def everywhere(stats, beside):
    for axis in ("tok", "vocab", "ckpt"):
        size, far = lax.axis_size(axis), 1
        while far < size:
            other = lax.ppermute(stats, axis, [(i, i ^ far) for i in range(size)])
            stats, far = combined(stats, other), far * 2
            if beside:
                stats = after(stats, beside.pop(0))
    return stats


def shards(heads, hidden, targets):
    ntok, nckpt, nvocab = (lax.axis_size(a) for a in ("tok", "ckpt", "vocab"))
    peers = nckpt * ntok
    mine = lax.axis_index("ckpt") * ntok + lax.axis_index("tok")
    rows = heads[0]
    depth, columns = rows.shape
    share = columns // peers
    wide = share // 128 * 128
    narrow = share - wide
    split = peers * wide
    per_device, features = hidden.shape[1:]
    tokens = per_device * ntok
    ckpts = nckpt
    fold = 4

    size = per_device // nvocab
    own = lax.dynamic_slice_in_dim(hidden[0], lax.axis_index("vocab") * size, size, 0)
    along = lax.all_gather(own, "ckpt", axis=0)

    wide_block, narrow_block = pack(rows, peers, wide, narrow, fold)
    narrow_in = exchange(narrow_block)
    states = lax.all_gather(after(staged(along), narrow_in), ("tok", "vocab"), axis=0)
    if size % 16:
        states = states.transpose(1, 0, 2, 3).reshape(1, ckpts, tokens, features)
    wide_in = exchange(after(wide_block, narrow_in))
    labels = lax.all_gather(after(targets, narrow_in), "tok", axis=0, tiled=True)[:, None]
    narrow_in = narrow_in.reshape(ckpts, ntok, depth // fold, fold * narrow)

    base = lax.axis_index("vocab") * columns
    ids = jnp.concatenate(
        [base + mine * wide + jnp.arange(wide), base + split + mine * narrow + jnp.arange(narrow)]
    ).astype(jnp.int32)[None]
    wide_logits, narrow_logits, stats = score(
        states, wide_in.reshape(ckpts, ntok * depth, wide), narrow_in, narrow, labels, ids
    )
    hidden_sq, hidden_rows, pieces = (), [], []
    for step in range(4):
        whole, part = squares(after(states, stats), hidden_sq, step, 4)
        hidden_sq = (whole,)
        hidden_rows.append(part)
        pieces.append(part)
    hidden_sq, hidden_rows = hidden_sq[0], sum(hidden_rows)
    top, total, squared, hit = everywhere(stats[:, :4].transpose(1, 0, 2), pieces)
    resid_rows = squared / (total * total) + jnp.square(hit / total - 1.0)
    vocab_total = columns * nvocab
    count = float(tokens * features * vocab_total)
    level = jnp.sum(hidden_rows[:, 0] * resid_rows, axis=1) / jnp.float32(count)
    scales = jnp.concatenate([1.0 / level, jnp.full((1,), vocab_total / tokens, jnp.float32)])
    table = jnp.concatenate([top, total]).T

    out = exchange(
        merge(
            scales, wide_logits, narrow_logits, table, labels, ids, hidden_sq,
            wide_in.reshape(ckpts, ntok, depth, wide), narrow_in, ntok,
        )
    )
    own_rows = depth // ntok
    height = own_rows // fold
    narrow_out = out[:, own_rows : own_rows + height].reshape(peers, height, fold, narrow).transpose(2, 1, 0, 3)
    return jnp.concatenate(
        [out[:, :own_rows].transpose(1, 0, 2).reshape(own_rows, -1), narrow_out.reshape(own_rows, -1)], axis=1
    )


def solution(mesh):
    placed = (P("ckpt", "tok", "vocab"), P("ckpt", "tok", None), P("tok"))
    return jax.shard_map(
        shards, mesh=mesh, in_specs=placed, out_specs=P(("ckpt", "tok"), "vocab"), check_vma=False
    )
```

```python
import functools
import math

import jax
import jax.numpy as jnp
from jax import lax
from jax.experimental import pallas as pl
from jax.experimental.pallas import tpu as pltpu
from jax.sharding import PartitionSpec as P

prior_weight = 0.05
VMEM = 56 * 1024 * 1024
BOTH = ("ckpt", "tok")


def call(kernel, name, **options):
    return pl.pallas_call(
        kernel, name=name, compiler_params=pltpu.CompilerParams(vmem_limit_bytes=VMEM), **options
    )


def pack_kernel(*refs):
    parts, out_ref = refs[:-1], refs[-1]
    peers, blocks, _, wide = out_ref.shape
    fold = len(parts)
    narrow = wide // fold
    split = peers * wide
    for g in range(peers):
        for q, part in enumerate(parts):
            out_ref[g, q] = part[:, g * wide : (g + 1) * wide]
        lo = split + g * narrow
        out_ref[g, fold] = jnp.concatenate([part[:, lo : lo + narrow] for part in parts], axis=1)


def pack(rows, peers, wide, fold):
    depth, columns = rows.shape
    height = depth // fold
    tall = 32
    steps = height // tall

    def part(q):
        return pl.BlockSpec((tall, columns), lambda i: (q * steps + i, 0))

    out = call(
        pack_kernel, "pack",
        out_shape=jax.ShapeDtypeStruct((peers, fold + 1, height, wide), rows.dtype),
        grid=(steps,),
        in_specs=[part(q) for q in range(fold)],
        out_specs=pl.BlockSpec((peers, fold + 1, tall, wide), lambda i: (0, 0, i, 0)),
    )(*([rows] * fold))
    return out.reshape(peers, depth + height, wide)


def squared(x):
    return jnp.square(x.astype(jnp.float32)).astype(jnp.bfloat16)


def rows_kernel(states_ref, out_ref):
    x = squared(states_ref[...].reshape(-1, states_ref.shape[3]))
    ones = jnp.ones((8, x.shape[1]), jnp.bfloat16)
    out_ref[0] = lax.dot_general(ones, x, (((1,), (1,)), ((), ())), preferred_element_type=jnp.float32)


def row_sums(states, features):
    groups, ckpts, size, _ = states.shape
    return call(
        rows_kernel, "rows",
        out_shape=jax.ShapeDtypeStruct((ckpts, 8, groups * size), jnp.float32),
        grid=(ckpts,),
        in_specs=[pl.BlockSpec((groups, 1, size, features), lambda c: (0, c, 0, 0))],
        out_specs=pl.BlockSpec((1, 8, groups * size), lambda c: (c, 0, 0)),
    )(states)


def unfolded(block, fold):
    w = block.shape[1] // fold
    return jnp.concatenate([block[:, q * w : (q + 1) * w] for q in range(fold)], axis=0)


def padded(blocks, lanes):
    x = jnp.concatenate(blocks, axis=0)
    return jnp.concatenate([x, jnp.zeros((x.shape[0], lanes - x.shape[1]), x.dtype)], axis=1)


def score_kernel(states_ref, heads_ref, labels_ref, ids_ref, logits_ref, stats_ref):
    states = states_ref[...].reshape(-1, states_ref.shape[3])
    blocks, _, wide = heads_ref.shape[1:]
    depth = states.shape[1] // blocks
    slim = logits_ref.shape[2] - wide
    fold = wide // (slim // 2)
    narrow = padded([unfolded(heads_ref[0, b, depth:], fold) for b in range(blocks)], slim)
    heads = jnp.concatenate([heads_ref[0, b, :depth] for b in range(blocks)], axis=0)
    x = jnp.concatenate(
        [jnp.dot(states, y, preferred_element_type=jnp.float32) for y in (heads, narrow)], axis=1
    )
    x = jnp.where(ids_ref[...] >= 0, x, -3e38)
    logits_ref[0] = x
    top = jnp.max(x, axis=1, keepdims=True)
    grown = jnp.exp(x - top)
    target = labels_ref[...] == ids_ref[...]
    mass = jnp.sum(grown, axis=1, keepdims=True)
    hit = jnp.sum(jnp.where(target, grown, 0.0), axis=1, keepdims=True)
    square = jnp.sum(jnp.where(target, 0.0, grown * grown), axis=1, keepdims=True)
    lane = lax.broadcasted_iota(jnp.int32, (top.shape[0], 128), 1)
    table = jnp.where(lane == 0, top, jnp.where(lane == 1, mass, jnp.where(lane == 2, square, hit)))
    stats_ref[0] = table.T[:8]


def score(states, features, heads, labels, ids):
    groups, ckpts, size, _ = states.shape
    tokens, lanes = groups * size, ids.shape[1]
    return call(
        score_kernel, "score",
        out_shape=(
            jax.ShapeDtypeStruct((ckpts, tokens, lanes), jnp.float32),
            jax.ShapeDtypeStruct((ckpts, 8, tokens), jnp.float32),
        ),
        grid=(ckpts,),
        in_specs=[
            pl.BlockSpec((groups, 1, size, features), lambda c: (0, c, 0, 0)),
            pl.BlockSpec((1, *heads.shape[1:]), lambda c: (c, 0, 0, 0)),
            pl.BlockSpec(labels.shape, lambda c: (0, 0)),
            pl.BlockSpec(ids.shape, lambda c: (0, 0)),
        ],
        out_specs=(
            pl.BlockSpec((1, tokens, lanes), lambda c: (c, 0, 0)),
            pl.BlockSpec((1, 8, tokens), lambda c: (c, 0, 0)),
        ),
    )(states, heads, labels, ids)


def merge_kernel(
    scale_ref, logits_ref, table_ref, labels_ref, ids_ref, hidden_ref, heads_ref, out_ref, resid_ref,
    *, prior
):
    ckpts = logits_ref.shape[0]
    wide, depth = heads_ref.shape[3], hidden_ref.shape[3]
    slim = logits_ref.shape[2] - wide
    fold = wide // (slim // 2)

    @pl.when(pl.program_id(0) == 0)
    def _():
        target = jnp.where(labels_ref[...] == ids_ref[...], 1.0, 0.0)
        for c in range(ckpts):
            top, total = table_ref[:, c : c + 1], table_ref[:, ckpts + c : ckpts + c + 1]
            share = jnp.exp(logits_ref[c] - top) * (1.0 / total)
            resid_ref[c] = jnp.square(share - target).astype(jnp.bfloat16)

    hidden = [squared(hidden_ref[:, c].reshape(-1, hidden_ref.shape[3])) for c in range(ckpts)]

    def blend(lo, hi, heads_of):
        numer = denom = None
        for c in range(ckpts):
            product = lax.dot_general(
                hidden[c], resid_ref[c, :, lo:hi], (((0,), (0,)), ((), ())), preferred_element_type=jnp.float32
            )
            weight = (product * scale_ref[c] + prior).astype(jnp.bfloat16).astype(jnp.float32)
            term = weight * heads_of(c).astype(jnp.float32)
            numer = term if numer is None else numer + term
            denom = weight if denom is None else denom + weight
        return numer / denom

    peers, own = out_ref.shape[0], depth // out_ref.shape[0]
    merged = blend(0, wide, lambda c: heads_ref[c, 0, :depth])
    out_ref[:, :own] = merged.astype(out_ref.dtype).reshape(peers, own, wide)
    merged = blend(wide, wide + slim, lambda c: padded([unfolded(heads_ref[c, 0, depth:], fold)], slim))
    height = own // fold
    for peer in range(peers):
        pieces = [
            merged[peer * own + q * height : peer * own + (q + 1) * height, : slim // 2] for q in range(fold)
        ]
        block = jnp.concatenate(pieces, axis=1)
        rest = jnp.zeros((out_ref.shape[1] - own - height, block.shape[1]), jnp.float32)
        out_ref[peer, own:] = jnp.concatenate([block, rest], axis=0).astype(out_ref.dtype)


def merge(scales, prior, logits, table, labels, ids, states, heads, depth, ntok):
    ckpts, blocks, _, width = heads.shape
    tokens, lanes = logits.shape[1:]
    slim = (lanes - width) // 2
    own = depth // ntok
    tall = own + -(-own * slim // width // 16) * 16

    def whole(x):
        return pl.BlockSpec(x.shape, lambda i: (0,) * x.ndim)

    return call(
        functools.partial(merge_kernel, prior=prior), "merge",
        out_shape=jax.ShapeDtypeStruct((blocks * ntok, tall, width), jnp.bfloat16),
        grid=(blocks,),
        in_specs=[pl.BlockSpec(memory_space=pltpu.SMEM)]
        + [whole(x) for x in (logits, table, labels, ids)]
        + [
            pl.BlockSpec((*states.shape[:3], depth), lambda i: (0, 0, 0, i)),
            pl.BlockSpec((ckpts, 1, *heads.shape[2:]), lambda i: (0, i, 0, 0)),
        ],
        out_specs=pl.BlockSpec((ntok, tall, width), lambda i: (i, 0, 0)),
        scratch_shapes=[pltpu.VMEM((ckpts, tokens, lanes), jnp.bfloat16)],
    )(scales, logits, table, labels, ids, states, heads)


def after(value, *earlier):
    return lax.optimization_barrier((value, *earlier))[0] if earlier else value


def exchange(x):
    return lax.all_to_all(x, BOTH, 0, 0, tiled=True)


def combined(x, y):
    top = jnp.maximum(x[0], y[0])
    fx, fy = jnp.exp(x[0] - top), jnp.exp(y[0] - top)
    return jnp.stack(
        [top, x[1] * fx + y[1] * fy, x[2] * (fx * fx) + y[2] * (fy * fy), x[3] * fx + y[3] * fy]
    )


def everywhere(stats):
    for axis in ("tok", "vocab", "ckpt"):
        size, far = lax.axis_size(axis), 1
        while far < size:
            other = lax.ppermute(stats, axis, [(i, i ^ far) for i in range(size)])
            stats, far = combined(stats, other), far * 2
    return stats


def shards(heads, hidden, targets):
    ntok, nckpt, nvocab = (lax.axis_size(a) for a in ("tok", "ckpt", "vocab"))
    peers = nckpt * ntok
    mine = lax.axis_index("ckpt") * ntok + lax.axis_index("tok")
    rows = heads[0]
    depth, columns = rows.shape
    share = columns // peers
    wide = share // 128 * 128
    narrow = share - wide
    split = peers * wide
    per_device, features = hidden.shape[1:]
    tokens = per_device * ntok
    ckpts = nckpt
    fold = 4

    size = per_device // nvocab
    own = lax.dynamic_slice_in_dim(hidden[0], lax.axis_index("vocab") * size, size, 0)
    label = lax.dynamic_slice_in_dim(targets, lax.axis_index("vocab") * size, size, 0)[:, None]
    digits = jnp.concatenate([label % 256, label // 256 % 256, label // 65536], axis=1)
    digits = jnp.pad(digits.astype(hidden.dtype), ((0, 0), (0, 125)))
    own = jnp.concatenate([own, digits], axis=1)[None]

    def other(x, axis, far):
        return lax.ppermute(x, axis, [(i, i ^ far) for i in range(lax.axis_size(axis))])

    def paired(x, y, axis, far):
        upper = lax.axis_index(axis) // far % 2 == 1
        return jnp.concatenate([jnp.where(upper, y, x), jnp.where(upper, x, y)])

    planes = [own] + [other(own, "ckpt", far) for far in (2, 3, 1)]
    packed = pack(rows, peers, wide, fold)
    columns_in = exchange(packed).reshape(ckpts, ntok, depth + depth // fold, wide)
    states = paired(
        paired(planes[0], planes[3], "ckpt", 1), paired(planes[1], planes[2], "ckpt", 1), "ckpt", 2
    )[None]
    states = after(states, packed)
    chains = [states, other(states, "tok", 2)]
    for i in (0, 1):
        far = 1
        while far < nvocab:
            chains[i] = paired(chains[i], other(chains[i], "vocab", far), "vocab", far)
            far *= 2
    states = paired(*chains, "tok", 2)
    states = paired(states, other(states, "tok", 1), "tok", 1)
    labels = states[:, 0, :, features : features + 3].reshape(tokens, 3).astype(jnp.int32)
    labels = labels[:, :1] + 256 * labels[:, 1:2] + 65536 * labels[:, 2:]
    if size % 16:
        states = states.transpose(1, 0, 2, 3).reshape(1, ckpts, tokens, features + 128)

    base = lax.axis_index("vocab") * columns
    pad = jnp.full((narrow,), -1)
    ids = jnp.concatenate(
        [base + mine * wide + jnp.arange(wide), base + split + mine * narrow + jnp.arange(narrow), pad]
    ).astype(jnp.int32)[None]
    hidden_rows = row_sums(states, features)
    logits, stats = score(after(states, hidden_rows), features, columns_in, labels, ids)
    top, total, off, hit = everywhere(stats[:, :4].transpose(1, 0, 2))
    resid_rows = off / (total * total) + jnp.square(hit / total - 1.0)
    vocab_total = columns * nvocab
    count = float(tokens * features * vocab_total)
    level = jnp.sum(hidden_rows[:, 0] * resid_rows, axis=1) / jnp.float32(count)
    ratio = vocab_total / tokens
    shrink = 2.0 ** -math.ceil(math.log2(max(ratio, 1.0)))
    scales = jnp.float32(ratio * shrink) / level
    table = jnp.concatenate([top, total]).T

    out = exchange(
        merge(
            scales, prior_weight * shrink, logits, table, labels, ids, states,
            columns_in, depth, ntok,
        )
    )
    own_rows = depth // ntok
    height = own_rows // fold
    narrow_out = out[:, own_rows : own_rows + height].reshape(peers, height, fold, narrow).transpose(2, 1, 0, 3)
    return jnp.concatenate(
        [out[:, :own_rows].transpose(1, 0, 2).reshape(own_rows, -1), narrow_out.reshape(own_rows, -1)], axis=1
    )


def solution(mesh):
    placed = (P("ckpt", "tok", "vocab"), P("ckpt", "tok", None), P("tok"))
    return jax.shard_map(
        shards, mesh=mesh, in_specs=placed, out_specs=P(("ckpt", "tok"), "vocab"), check_vma=False
    )
```

```python
import functools
import math

import jax
import jax.numpy as jnp
from jax import lax
from jax.experimental import pallas as pl
from jax.experimental.pallas import tpu as pltpu
from jax.sharding import PartitionSpec as P

prior_weight = 0.05
VMEM = 56 * 1024 * 1024
BOTH = ("ckpt", "tok")


def call(kernel, name, vmem=VMEM, **options):
    return pl.pallas_call(
        kernel, name=name, compiler_params=pltpu.CompilerParams(vmem_limit_bytes=vmem), **options
    )


def pack_kernel(*refs):
    parts, out_ref = refs[:-1], refs[-1]
    peers, blocks, _, wide = out_ref.shape
    fold = len(parts)
    narrow = wide // fold
    split = peers * wide
    for g in range(peers):
        for q, part in enumerate(parts):
            out_ref[g, q] = part[:, g * wide : (g + 1) * wide]
        lo = split + g * narrow
        out_ref[g, fold] = jnp.concatenate([part[:, lo : lo + narrow] for part in parts], axis=1)


def pack(rows, peers, wide, fold):
    depth, columns = rows.shape
    height = depth // fold
    tall = 32
    steps = height // tall

    def part(q):
        return pl.BlockSpec((tall, columns), lambda i: (q * steps + i, 0))

    out = call(
        pack_kernel, "pack",
        out_shape=jax.ShapeDtypeStruct((peers, fold + 1, height, wide), rows.dtype),
        grid=(steps,),
        in_specs=[part(q) for q in range(fold)],
        out_specs=pl.BlockSpec((peers, fold + 1, tall, wide), lambda i: (0, 0, i, 0)),
    )(*([rows] * fold))
    return out.reshape(peers, depth + height, wide)


def squared(x):
    return jnp.square(x.astype(jnp.float32)).astype(jnp.bfloat16)


def square_kernel(states_ref, out_ref, sum_ref):
    turned = squared(states_ref[...].reshape(-1, states_ref.shape[3])).T
    out_ref[0] = turned
    part = jnp.sum(turned.astype(jnp.float32), axis=0, keepdims=True)

    @pl.when(pl.program_id(1) == 0)
    def _():
        sum_ref[0] = part

    @pl.when(pl.program_id(1) > 0)
    def _():
        sum_ref[0] += part


def squares(states, features, blocks):
    groups, ckpts, size, _ = states.shape
    tokens, tile = groups * size, features // blocks
    return call(
        square_kernel, "squares",
        out_shape=(
            jax.ShapeDtypeStruct((ckpts, features, tokens), jnp.bfloat16),
            jax.ShapeDtypeStruct((ckpts, 1, tokens), jnp.float32),
        ),
        grid=(ckpts, blocks),
        in_specs=[pl.BlockSpec((groups, 1, size, tile), lambda c, f: (0, c, 0, f))],
        out_specs=(
            pl.BlockSpec((1, tile, tokens), lambda c, f: (c, f, 0)),
            pl.BlockSpec((1, 1, tokens), lambda c, f: (c, 0, 0)),
        ),
    )(states)


def unfolded(block, fold):
    w = block.shape[1] // fold
    return jnp.concatenate([block[:, q * w : (q + 1) * w] for q in range(fold)], axis=0)


def padded(blocks, lanes):
    x = jnp.concatenate(blocks, axis=0)
    return jnp.concatenate([x, jnp.zeros((x.shape[0], lanes - x.shape[1]), x.dtype)], axis=1)


def score_kernel(states_ref, heads_ref, labels_ref, ids_ref, logits_ref, stats_ref):
    states = states_ref[...].reshape(-1, states_ref.shape[3])
    blocks, _, wide = heads_ref.shape[1:]
    depth = states.shape[1] // blocks
    slim = logits_ref.shape[2] - wide
    fold = wide // (slim // 2)
    narrow = padded([unfolded(heads_ref[0, b, depth:], fold) for b in range(blocks)], slim)
    heads = jnp.concatenate([heads_ref[0, b, :depth] for b in range(blocks)], axis=0)
    x = jnp.concatenate(
        [jnp.dot(states, y, preferred_element_type=jnp.float32) for y in (heads, narrow)], axis=1
    )
    x = jnp.where(ids_ref[...] >= 0, x, -3e38)
    logits_ref[0] = x
    top = jnp.max(x, axis=1, keepdims=True)
    grown = jnp.exp(x - top)
    target = labels_ref[...] == ids_ref[...]
    mass = jnp.sum(grown, axis=1, keepdims=True)
    hit = jnp.sum(jnp.where(target, grown, 0.0), axis=1, keepdims=True)
    square = jnp.sum(jnp.where(target, 0.0, grown * grown), axis=1, keepdims=True)
    lane = lax.broadcasted_iota(jnp.int32, (top.shape[0], 128), 1)
    table = jnp.where(lane == 0, top, jnp.where(lane == 1, mass, jnp.where(lane == 2, square, hit)))
    stats_ref[0] = table.T[:8]


def score(states, features, heads, labels, ids):
    groups, ckpts, size, _ = states.shape
    tokens, lanes = groups * size, ids.shape[1]
    return call(
        score_kernel, "score",
        out_shape=(
            jax.ShapeDtypeStruct((ckpts, tokens, lanes), jnp.float32),
            jax.ShapeDtypeStruct((ckpts, 8, tokens), jnp.float32),
        ),
        grid=(ckpts,),
        in_specs=[
            pl.BlockSpec((groups, 1, size, features), lambda c: (0, c, 0, 0)),
            pl.BlockSpec((1, *heads.shape[1:]), lambda c: (c, 0, 0, 0)),
            pl.BlockSpec(labels.shape, lambda c: (0, 0)),
            pl.BlockSpec(ids.shape, lambda c: (0, 0)),
        ],
        out_specs=(
            pl.BlockSpec((1, tokens, lanes), lambda c: (c, 0, 0)),
            pl.BlockSpec((1, 8, tokens), lambda c: (c, 0, 0)),
        ),
    )(states, heads, labels, ids)


def merge_kernel(
    place_ref, scale_ref, logits_ref, table_ref, labels_ref, ids_ref, hidden_ref, heads_ref, *refs, prior
):
    outs, wide_rows, slim_rows, resid_ref = refs[:-3], *refs[-3:]
    ckpts, tokens, lanes = resid_ref.shape
    wide, depth = heads_ref.shape[3], hidden_ref.shape[1]
    slim = lanes - wide
    fold = wide // (slim // 2)

    @pl.when(pl.program_id(0) == 0)
    def _():
        target = jnp.where(labels_ref[...] == ids_ref[...], 1.0, 0.0)
        table = table_ref[...].T
        for c in range(ckpts):
            top, total = table[:, c : c + 1], table[:, ckpts + c : ckpts + c + 1]
            share = jnp.exp(logits_ref[c] - top) * (1.0 / total)
            resid_ref[c] = jnp.square(share - target).astype(jnp.bfloat16)

    def blend(lo, hi, heads_of):
        numer = denom = None
        for c in range(ckpts):
            product = jnp.dot(hidden_ref[c], resid_ref[c, :, lo:hi], preferred_element_type=jnp.float32)
            weight = (product * scale_ref[c] + prior).astype(jnp.bfloat16).astype(jnp.float32)
            term = weight * heads_of(c).astype(jnp.float32)
            numer = term if numer is None else numer + term
            denom = weight if denom is None else denom + weight
        return numer / denom

    wide_rows[...] = blend(0, wide, lambda c: heads_ref[c, 0, :depth])
    slim_rows[...] = blend(wide, lanes, lambda c: padded([unfolded(heads_ref[c, 0, depth:], fold)], slim))
    pair = outs[0].shape[0]
    halves = len(outs) // ckpts
    own = depth // (pair * halves)
    height = own // fold
    for plane in range(ckpts):

        @pl.when(pl.program_id(0) == plane)
        def _():
            for far in range(pair * halves):
                out_ref, slot = outs[plane * halves + far // pair], far % pair
                first = pl.multiple_of((place_ref[1] ^ far) * own, own)
                out_ref[slot, :own] = wide_rows[pl.ds(first, own)].astype(out_ref.dtype)
                rows = slim_rows[pl.ds(first, own)]
                block = jnp.concatenate(
                    [rows[q * height : (q + 1) * height, : slim // 2] for q in range(fold)], axis=1
                )
                rest = jnp.zeros((out_ref.shape[1] - own - height, wide), jnp.float32)
                out_ref[slot, own:] = jnp.concatenate([block, rest], axis=0).astype(out_ref.dtype)


def merge(place, scales, prior, logits, table, labels, ids, hidden_sq, heads, ntok):
    ckpts, blocks, _, width = heads.shape
    tokens, lanes = logits.shape[1:]
    depth = hidden_sq.shape[1] // blocks
    own = depth // ntok
    tall = own + -(-own * (lanes - width) // 2 // width // 16) * 16
    shape = (2, tall, width)

    def whole(x):
        return pl.BlockSpec(x.shape, lambda i, s: (0,) * x.ndim)

    return call(
        functools.partial(merge_kernel, prior=prior), "merge",
        out_shape=[jax.ShapeDtypeStruct(shape, jnp.bfloat16)] * (blocks * ntok // 2),
        grid_spec=pltpu.PrefetchScalarGridSpec(
            num_scalar_prefetch=1,
            grid=(blocks,),
            in_specs=[pl.BlockSpec(memory_space=pltpu.SMEM)]
            + [whole(x) for x in (logits, table, labels, ids)]
            + [
                pl.BlockSpec((ckpts, depth, tokens), lambda i, s: (0, s[0] ^ i, 0)),
                pl.BlockSpec((ckpts, 1, *heads.shape[2:]), lambda i, s: (0, s[0] ^ i, 0, 0)),
            ],
            out_specs=[pl.BlockSpec(shape, lambda i, s: (0, 0, 0))] * (blocks * ntok // 2),
            scratch_shapes=[
                pltpu.VMEM((depth, width), jnp.float32),
                pltpu.VMEM((depth, lanes - width), jnp.float32),
                pltpu.VMEM((ckpts, tokens, lanes), jnp.bfloat16),
            ],
        ),
    )(place, scales, logits, table, labels, ids, hidden_sq, heads)


def assemble_kernel(mine_ref, *refs, sources):
    arrays, out_ref = refs[:-1], refs[-1]
    own, columns = out_ref.shape
    wide = arrays[0].shape[2]
    narrow = columns // len(sources) - wide
    fold = wide // narrow
    height = own // fold
    mine = mine_ref[0]
    slim = []
    for r, (array, slot) in enumerate(sources):
        out_ref[:, pl.ds(pl.multiple_of((mine ^ r) * wide, wide), wide)] = arrays[array][slot, :own]
        slim.append(unfolded(arrays[array][slot, own:].astype(jnp.float32)[:height], fold))
    for r in range(0, len(sources), 2):
        ours, theirs = slim[r], slim[r + 1]
        odd = mine % 2 == 1
        pair = jnp.concatenate([jnp.where(odd, theirs, ours), jnp.where(odd, ours, theirs)], axis=1)
        first = len(sources) * wide + (mine ^ r) // 2 * 2 * narrow
        out_ref[:, pl.ds(pl.multiple_of(first, 2 * narrow), 2 * narrow)] = pair.astype(out_ref.dtype)


def assemble(mine, arrays, sources, own, columns):
    return call(
        functools.partial(assemble_kernel, sources=sources), "assemble", VMEM // 2,
        out_shape=jax.ShapeDtypeStruct((own, columns), jnp.bfloat16),
        in_specs=[pl.BlockSpec(memory_space=pltpu.SMEM)] + [pl.BlockSpec(memory_space=pltpu.VMEM)] * len(arrays),
        out_specs=pl.BlockSpec(memory_space=pltpu.VMEM),
    )(mine.astype(jnp.int32)[None], *arrays)


def after(value, *earlier):
    return lax.optimization_barrier((value, *earlier))[0] if earlier else value


def exchange(x):
    return lax.all_to_all(x, BOTH, 0, 0, tiled=True)


def combined(x, y):
    top = jnp.maximum(x[0], y[0])
    fx, fy = jnp.exp(x[0] - top), jnp.exp(y[0] - top)
    return jnp.stack(
        [top, x[1] * fx + y[1] * fy, x[2] * (fx * fx) + y[2] * (fy * fy), x[3] * fx + y[3] * fy]
    )


def everywhere(stats):
    for axis in ("tok", "vocab", "ckpt"):
        size, far = lax.axis_size(axis), 1
        while far < size:
            other = lax.ppermute(stats, axis, [(i, i ^ far) for i in range(size)])
            stats, far = combined(stats, other), far * 2
    return stats


def shards(heads, hidden, targets):
    ntok, nckpt, nvocab = (lax.axis_size(a) for a in ("tok", "ckpt", "vocab"))
    peers = nckpt * ntok
    mine = lax.axis_index("ckpt") * ntok + lax.axis_index("tok")
    rows = heads[0]
    depth, columns = rows.shape
    share = columns // peers
    wide = share // 128 * 128
    narrow = share - wide
    split = peers * wide
    per_device, features = hidden.shape[1:]
    tokens = per_device * ntok
    ckpts = nckpt
    fold = 4

    size = per_device // nvocab
    own = lax.dynamic_slice_in_dim(hidden[0], lax.axis_index("vocab") * size, size, 0)
    label = lax.dynamic_slice_in_dim(targets, lax.axis_index("vocab") * size, size, 0)[:, None]
    digits = jnp.concatenate([label % 256, label // 256 % 256, label // 65536], axis=1)
    digits = jnp.pad(digits.astype(hidden.dtype), ((0, 0), (0, 125)))
    own = jnp.concatenate([own, digits], axis=1)[None]

    def other(x, axis, far):
        return lax.ppermute(x, axis, [(i, i ^ far) for i in range(lax.axis_size(axis))])

    def paired(x, y, axis, far):
        upper = lax.axis_index(axis) // far % 2 == 1
        return jnp.concatenate([jnp.where(upper, y, x), jnp.where(upper, x, y)])

    planes = [own] + [other(own, "ckpt", far) for far in (2, 3, 1)]
    packed = pack(rows, peers, wide, fold)
    columns_in = exchange(packed).reshape(ckpts, ntok, depth + depth // fold, wide)
    states = paired(
        paired(planes[0], planes[3], "ckpt", 1), paired(planes[1], planes[2], "ckpt", 1), "ckpt", 2
    )[None]
    states = after(states, packed)
    chains = [states, other(states, "tok", 2)]
    for i in (0, 1):
        far = 1
        while far < nvocab:
            chains[i] = paired(chains[i], other(chains[i], "vocab", far), "vocab", far)
            far *= 2
    states = paired(*chains, "tok", 2)
    states = paired(states, other(states, "tok", 1), "tok", 1)
    labels = states[:, 0, :, features : features + 3].reshape(tokens, 3).astype(jnp.int32)
    labels = labels[:, :1] + 256 * labels[:, 1:2] + 65536 * labels[:, 2:]
    if size % 16:
        states = states.transpose(1, 0, 2, 3).reshape(1, ckpts, tokens, features + 128)

    base = lax.axis_index("vocab") * columns
    pad = jnp.full((narrow,), -1)
    ids = jnp.concatenate(
        [base + mine * wide + jnp.arange(wide), base + split + mine * narrow + jnp.arange(narrow), pad]
    ).astype(jnp.int32)[None]
    hidden_sq, hidden_rows = squares(states, features, ntok)
    logits, stats = score(after(states, hidden_rows), features, columns_in, labels, ids)
    top, total, off, hit = everywhere(stats[:, :4].transpose(1, 0, 2))
    resid_rows = off / (total * total) + jnp.square(hit / total - 1.0)
    vocab_total = columns * nvocab
    count = float(tokens * features * vocab_total)
    level = jnp.sum(hidden_rows[:, 0] * resid_rows, axis=1) / jnp.float32(count)
    ratio = vocab_total / tokens
    shrink = 2.0 ** -math.ceil(math.log2(max(ratio, 1.0)))
    scales = jnp.float32(ratio * shrink) / level
    table = jnp.concatenate([top, total])

    place = jnp.stack([lax.axis_index("ckpt"), lax.axis_index("tok")]).astype(jnp.int32)
    parts = merge(
        place, scales, prior_weight * shrink, logits, table, labels, ids, hidden_sq, columns_in, ntok
    )
    arrays, sources, seconds = [], {}, []
    for half in reversed(range(peers // 2)):
        r, part = 2 * half, parts[half]
        if r:
            part = lax.ppermute(part, BOTH, [(g, g ^ r) for g in range(peers)])
        sources[r] = (len(arrays), 0)
        arrays.append(part)
        seconds.append((r + 1, part))
        if half in (peers // 4, 0):
            handed = other(jnp.stack([x[1] for _, x in seconds]), "tok", 1)
            for slot, (s, _) in enumerate(seconds):
                sources[s] = (len(arrays), slot)
            arrays.append(handed)
            seconds = []
    return assemble(mine, arrays, [sources[r] for r in range(peers)], depth // ntok, columns)


def solution(mesh):
    placed = (P("ckpt", "tok", "vocab"), P("ckpt", "tok", None), P("tok"))
    return jax.shard_map(
        shards, mesh=mesh, in_specs=placed, out_specs=P(("ckpt", "tok"), "vocab"), check_vma=False
    )
```

```python
import functools
import math

import jax
import jax.numpy as jnp
from jax import lax
from jax.experimental import pallas as pl
from jax.experimental.pallas import tpu as pltpu
from jax.sharding import PartitionSpec as P

prior_weight = 0.05
VMEM = 30 * 1024 * 1024
BOTH = ("ckpt", "tok")


def call(kernel, name, vmem=VMEM, **options):
    return pl.pallas_call(
        kernel, name=name, compiler_params=pltpu.CompilerParams(vmem_limit_bytes=vmem), **options
    )


def in_hbm(x):
    return pltpu.with_memory_space_constraint(x, pltpu.HBM)


def pack_kernel(*refs):
    parts, out_ref = refs[:-1], refs[-1]
    peers, blocks, _, wide = out_ref.shape
    fold = len(parts)
    narrow = wide // fold
    split = peers * wide
    for g in range(peers):
        for q, part in enumerate(parts):
            out_ref[g, q] = part[:, g * wide : (g + 1) * wide]
        lo = split + g * narrow
        out_ref[g, fold] = jnp.concatenate([part[:, lo : lo + narrow] for part in parts], axis=1)


def pack(rows, peers, wide, fold):
    depth, columns = rows.shape
    height = depth // fold
    tall = 32
    steps = height // tall

    def part(q):
        return pl.BlockSpec((tall, columns), lambda i: (q * steps + i, 0))

    out = call(
        pack_kernel, "pack",
        out_shape=jax.ShapeDtypeStruct((peers, fold + 1, height, wide), rows.dtype),
        grid=(steps,),
        in_specs=[part(q) for q in range(fold)],
        out_specs=pl.BlockSpec((peers, fold + 1, tall, wide), lambda i: (0, 0, i, 0)),
    )(*([in_hbm(rows)] * fold))
    return out.reshape(peers, depth + height, wide)


def squared(x):
    return jnp.square(x.astype(jnp.float32)).astype(jnp.bfloat16)


def square_kernel(states_ref, out_ref, sum_ref):
    turned = squared(states_ref[...].reshape(-1, states_ref.shape[3])).T
    out_ref[0] = turned
    part = jnp.sum(turned.astype(jnp.float32), axis=0, keepdims=True)

    @pl.when(pl.program_id(1) == 0)
    def _():
        sum_ref[0] = part

    @pl.when(pl.program_id(1) > 0)
    def _():
        sum_ref[0] += part


def squares(states, features, blocks):
    groups, ckpts, size, _ = states.shape
    tokens, tile = groups * size, features // blocks
    return call(
        square_kernel, "squares",
        out_shape=(
            jax.ShapeDtypeStruct((ckpts, features, tokens), jnp.bfloat16),
            jax.ShapeDtypeStruct((ckpts, 1, tokens), jnp.float32),
        ),
        grid=(ckpts, blocks),
        in_specs=[pl.BlockSpec((groups, 1, size, tile), lambda c, f: (0, c, 0, f))],
        out_specs=(
            pl.BlockSpec((1, tile, tokens), lambda c, f: (c, f, 0)),
            pl.BlockSpec((1, 1, tokens), lambda c, f: (c, 0, 0)),
        ),
    )(states)


def unfolded(block, fold):
    w = block.shape[1] // fold
    return jnp.concatenate([block[:, q * w : (q + 1) * w] for q in range(fold)], axis=0)


def padded(blocks, lanes):
    x = jnp.concatenate(blocks, axis=0)
    return jnp.concatenate([x, jnp.zeros((x.shape[0], lanes - x.shape[1]), x.dtype)], axis=1)


def score_kernel(states_ref, heads_ref, labels_ref, ids_ref, logits_ref, stats_ref):
    states = states_ref[...].reshape(-1, states_ref.shape[3])
    blocks, _, wide = heads_ref.shape[1:]
    depth = states.shape[1] // blocks
    slim = logits_ref.shape[2] - wide
    fold = wide // (slim // 2)
    narrow = padded([unfolded(heads_ref[0, b, depth:], fold) for b in range(blocks)], slim)
    heads = jnp.concatenate([heads_ref[0, b, :depth] for b in range(blocks)], axis=0)
    x = jnp.concatenate(
        [jnp.dot(states, y, preferred_element_type=jnp.float32) for y in (heads, narrow)], axis=1
    )
    x = jnp.where(ids_ref[...] >= 0, x, -3e38)
    logits_ref[0] = x
    top = jnp.max(x, axis=1, keepdims=True)
    grown = jnp.exp(x - top)
    target = labels_ref[...] == ids_ref[...]
    mass = jnp.sum(grown, axis=1, keepdims=True)
    hit = jnp.sum(jnp.where(target, grown, 0.0), axis=1, keepdims=True)
    square = jnp.sum(jnp.where(target, 0.0, grown * grown), axis=1, keepdims=True)
    lane = lax.broadcasted_iota(jnp.int32, (top.shape[0], 128), 1)
    table = jnp.where(lane == 0, top, jnp.where(lane == 1, mass, jnp.where(lane == 2, square, hit)))
    stats_ref[0] = table.T[:8]


def score(states, features, heads, labels, ids):
    groups, ckpts, size, _ = states.shape
    tokens, lanes = groups * size, ids.shape[1]
    return call(
        score_kernel, "score",
        out_shape=(
            pltpu.HBM((ckpts, tokens, lanes), jnp.float32),
            jax.ShapeDtypeStruct((ckpts, 8, tokens), jnp.float32),
        ),
        grid=(ckpts,),
        in_specs=[
            pl.BlockSpec((groups, 1, size, features), lambda c: (0, c, 0, 0)),
            pl.BlockSpec((1, *heads.shape[1:]), lambda c: (c, 0, 0, 0)),
            pl.BlockSpec(labels.shape, lambda c: (0, 0)),
            pl.BlockSpec(ids.shape, lambda c: (0, 0)),
        ],
        out_specs=(
            pl.BlockSpec((1, tokens, lanes), lambda c: (c, 0, 0)),
            pl.BlockSpec((1, 8, tokens), lambda c: (c, 0, 0)),
        ),
    )(in_hbm(states), in_hbm(heads), labels, ids)


def merge_kernel(
    place_ref, scale_ref, logits_ref, table_ref, labels_ref, ids_ref, hidden_ref, heads_ref, *refs, prior
):
    outs, wide_rows, slim_rows, resid_ref = refs[:-3], *refs[-3:]
    ckpts, tokens, lanes = resid_ref.shape
    wide, depth = heads_ref.shape[3], hidden_ref.shape[1]
    slim = lanes - wide
    fold = wide // (slim // 2)

    @pl.when(pl.program_id(0) == 0)
    def _():
        target = jnp.where(labels_ref[...] == ids_ref[...], 1.0, 0.0)
        table = table_ref[...].T
        for c in range(ckpts):
            top, total = table[:, c : c + 1], table[:, ckpts + c : ckpts + c + 1]
            share = jnp.exp(logits_ref[c] - top) * (1.0 / total)
            resid_ref[c] = jnp.square(share - target).astype(jnp.bfloat16)

    def blend(lo, hi, heads_of):
        numer = denom = None
        for c in range(ckpts):
            product = jnp.dot(hidden_ref[c], resid_ref[c, :, lo:hi], preferred_element_type=jnp.float32)
            weight = (product * scale_ref[c] + prior).astype(jnp.bfloat16).astype(jnp.float32)
            term = weight * heads_of(c).astype(jnp.float32)
            numer = term if numer is None else numer + term
            denom = weight if denom is None else denom + weight
        return numer / denom

    wide_rows[...] = blend(0, wide, lambda c: heads_ref[c, 0, :depth])
    slim_rows[...] = blend(wide, lanes, lambda c: padded([unfolded(heads_ref[c, 0, depth:], fold)], slim))
    pair = outs[0].shape[0]
    halves = len(outs) // ckpts
    own = depth // (pair * halves)
    height = own // fold
    for plane in range(ckpts):

        @pl.when(pl.program_id(0) == plane)
        def _():
            for far in range(pair * halves):
                out_ref, slot = outs[plane * halves + far // pair], far % pair
                first = pl.multiple_of((place_ref[1] ^ far) * own, own)
                out_ref[slot, :own] = wide_rows[pl.ds(first, own)].astype(out_ref.dtype)
                rows = slim_rows[pl.ds(first, own)]
                block = jnp.concatenate(
                    [rows[q * height : (q + 1) * height, : slim // 2] for q in range(fold)], axis=1
                )
                rest = jnp.zeros((out_ref.shape[1] - own - height, wide), jnp.float32)
                out_ref[slot, own:] = jnp.concatenate([block, rest], axis=0).astype(out_ref.dtype)


def merge(place, scales, prior, logits, table, labels, ids, hidden_sq, heads, ntok):
    ckpts, blocks, _, width = heads.shape
    tokens, lanes = logits.shape[1:]
    depth = hidden_sq.shape[1] // blocks
    own = depth // ntok
    tall = own + -(-own * (lanes - width) // 2 // width // 16) * 16
    shape = (2, tall, width)

    def whole(x):
        return pl.BlockSpec(x.shape, lambda i, s: (0,) * x.ndim)

    return call(
        functools.partial(merge_kernel, prior=prior), "merge",
        out_shape=[jax.ShapeDtypeStruct(shape, jnp.bfloat16)] * (blocks * ntok // 2),
        grid_spec=pltpu.PrefetchScalarGridSpec(
            num_scalar_prefetch=1,
            grid=(blocks,),
            in_specs=[pl.BlockSpec(memory_space=pltpu.SMEM)]
            + [whole(x) for x in (logits, table, labels, ids)]
            + [
                pl.BlockSpec((ckpts, depth, tokens), lambda i, s: (0, s[0] ^ i, 0)),
                pl.BlockSpec((ckpts, 1, *heads.shape[2:]), lambda i, s: (0, s[0] ^ i, 0, 0)),
            ],
            out_specs=[pl.BlockSpec(shape, lambda i, s: (0, 0, 0))] * (blocks * ntok // 2),
            scratch_shapes=[
                pltpu.VMEM((depth, width), jnp.float32),
                pltpu.VMEM((depth, lanes - width), jnp.float32),
                pltpu.VMEM((ckpts, tokens, lanes), jnp.bfloat16),
            ],
        ),
    )(place, scales, in_hbm(logits), table, labels, ids, hidden_sq, in_hbm(heads))


def assemble_kernel(mine_ref, *refs, sources):
    arrays, out_ref = refs[:-1], refs[-1]
    own, columns = out_ref.shape
    wide = arrays[0].shape[2]
    narrow = columns // len(sources) - wide
    fold = wide // narrow
    height = own // fold
    mine = mine_ref[0]
    slim = []
    for r, (array, slot) in enumerate(sources):
        out_ref[:, pl.ds(pl.multiple_of((mine ^ r) * wide, wide), wide)] = arrays[array][slot, :own]
        slim.append(unfolded(arrays[array][slot, own:].astype(jnp.float32)[:height], fold))
    for r in range(0, len(sources), 2):
        ours, theirs = slim[r], slim[r + 1]
        odd = mine % 2 == 1
        pair = jnp.concatenate([jnp.where(odd, theirs, ours), jnp.where(odd, ours, theirs)], axis=1)
        first = len(sources) * wide + (mine ^ r) // 2 * 2 * narrow
        out_ref[:, pl.ds(pl.multiple_of(first, 2 * narrow), 2 * narrow)] = pair.astype(out_ref.dtype)


def assemble(mine, arrays, sources, own, columns):
    return call(
        functools.partial(assemble_kernel, sources=sources), "assemble",
        out_shape=jax.ShapeDtypeStruct((own, columns), jnp.bfloat16),
        in_specs=[pl.BlockSpec(memory_space=pltpu.SMEM)] + [pl.BlockSpec(memory_space=pltpu.VMEM)] * len(arrays),
        out_specs=pl.BlockSpec(memory_space=pltpu.VMEM),
    )(mine.astype(jnp.int32)[None], *arrays)


def after(value, *earlier):
    return lax.optimization_barrier((value, *earlier))[0] if earlier else value


def exchange(x):
    return lax.all_to_all(x, BOTH, 0, 0, tiled=True)


def combined(x, y):
    top = jnp.maximum(x[0], y[0])
    fx, fy = jnp.exp(x[0] - top), jnp.exp(y[0] - top)
    return jnp.stack(
        [top, x[1] * fx + y[1] * fy, x[2] * (fx * fx) + y[2] * (fy * fy), x[3] * fx + y[3] * fy]
    )


def everywhere(stats):
    for axis in ("tok", "vocab", "ckpt"):
        size, far = lax.axis_size(axis), 1
        while far < size:
            other = lax.ppermute(stats, axis, [(i, i ^ far) for i in range(size)])
            stats, far = combined(stats, other), far * 2
    return stats


def shards(heads, hidden, targets):
    ntok, nckpt, nvocab = (lax.axis_size(a) for a in ("tok", "ckpt", "vocab"))
    peers = nckpt * ntok
    mine = lax.axis_index("ckpt") * ntok + lax.axis_index("tok")
    rows = heads[0]
    depth, columns = rows.shape
    share = columns // peers
    wide = share // 128 * 128
    narrow = share - wide
    split = peers * wide
    per_device, features = hidden.shape[1:]
    tokens = per_device * ntok
    ckpts = nckpt
    fold = 4

    size = per_device // nvocab
    own = lax.dynamic_slice_in_dim(hidden[0], lax.axis_index("vocab") * size, size, 0)
    label = lax.dynamic_slice_in_dim(targets, lax.axis_index("vocab") * size, size, 0)[:, None]
    digits = jnp.concatenate([label % 256, label // 256 % 256, label // 65536], axis=1)
    digits = jnp.pad(digits.astype(hidden.dtype), ((0, 0), (0, 125)))
    own = jnp.concatenate([own, digits], axis=1)[None]

    def other(x, axis, far):
        return lax.ppermute(x, axis, [(i, i ^ far) for i in range(lax.axis_size(axis))])

    def paired(x, y, axis, far):
        upper = lax.axis_index(axis) // far % 2 == 1
        return jnp.concatenate([jnp.where(upper, y, x), jnp.where(upper, x, y)])

    planes = [own] + [other(own, "ckpt", far) for far in (2, 3, 1)]
    packed = pack(rows, peers, wide, fold)
    columns_in = exchange(packed).reshape(ckpts, ntok, depth + depth // fold, wide)
    states = paired(
        paired(planes[0], planes[3], "ckpt", 1), paired(planes[1], planes[2], "ckpt", 1), "ckpt", 2
    )[None]
    states = after(states, packed)
    chains = [states, other(states, "tok", 2)]
    for i in (0, 1):
        far = 1
        while far < nvocab:
            chains[i] = paired(chains[i], other(chains[i], "vocab", far), "vocab", far)
            far *= 2
    states = paired(*chains, "tok", 2)
    states = paired(states, other(states, "tok", 1), "tok", 1)
    labels = states[:, 0, :, features : features + 3].reshape(tokens, 3).astype(jnp.int32)
    labels = labels[:, :1] + 256 * labels[:, 1:2] + 65536 * labels[:, 2:]
    if size % 16:
        states = states.transpose(1, 0, 2, 3).reshape(1, ckpts, tokens, features + 128)

    base = lax.axis_index("vocab") * columns
    pad = jnp.full((narrow,), -1)
    ids = jnp.concatenate(
        [base + mine * wide + jnp.arange(wide), base + split + mine * narrow + jnp.arange(narrow), pad]
    ).astype(jnp.int32)[None]
    hidden_sq, hidden_rows = squares(states, features, ntok)
    logits, stats = score(after(states, hidden_rows), features, columns_in, labels, ids)
    top, total, off, hit = everywhere(stats[:, :4].transpose(1, 0, 2))
    resid_rows = off / (total * total) + jnp.square(hit / total - 1.0)
    vocab_total = columns * nvocab
    count = float(tokens * features * vocab_total)
    level = jnp.sum(hidden_rows[:, 0] * resid_rows, axis=1) / jnp.float32(count)
    ratio = vocab_total / tokens
    shrink = 2.0 ** -math.ceil(math.log2(max(ratio, 1.0)))
    scales = jnp.float32(ratio * shrink) / level
    table = jnp.concatenate([top, total])

    place = jnp.stack([lax.axis_index("ckpt"), lax.axis_index("tok")]).astype(jnp.int32)
    parts = merge(
        place, scales, prior_weight * shrink, logits, table, labels, ids, hidden_sq, columns_in, ntok
    )
    arrays, sources, seconds = [], {}, []
    for half in reversed(range(peers // 2)):
        r, part = 2 * half, parts[half]
        if r:
            part = lax.ppermute(part, BOTH, [(g, g ^ r) for g in range(peers)])
        sources[r] = (len(arrays), 0)
        arrays.append(part)
        seconds.append((r + 1, part))
        if half in (peers // 4, 0):
            handed = other(jnp.stack([x[1] for _, x in seconds]), "tok", 1)
            for slot, (s, _) in enumerate(seconds):
                sources[s] = (len(arrays), slot)
            arrays.append(handed)
            seconds = []
    return assemble(mine, arrays, [sources[r] for r in range(peers)], depth // ntok, columns)


def solution(mesh):
    placed = (P("ckpt", "tok", "vocab"), P("ckpt", "tok", None), P("tok"))
    return jax.shard_map(
        shards, mesh=mesh, in_specs=placed, out_specs=P(("ckpt", "tok"), "vocab"), check_vma=False
    )
```

```python
import functools
import math

import jax
import jax.numpy as jnp
from jax import lax
from jax.experimental import pallas as pl
from jax.experimental.pallas import tpu as pltpu
from jax.sharding import PartitionSpec as P

prior_weight = 0.05
VMEM = 30 * 1024 * 1024
BOTH = ("ckpt", "tok")


def call(kernel, name, vmem=VMEM, **options):
    return pl.pallas_call(
        kernel, name=name, compiler_params=pltpu.CompilerParams(vmem_limit_bytes=vmem), **options
    )


def in_hbm(x):
    return pltpu.with_memory_space_constraint(x, pltpu.HBM)


def pack_kernel(*refs):
    parts, out_ref = refs[:-1], refs[-1]
    peers, blocks, _, wide = out_ref.shape
    fold = len(parts)
    narrow = wide // fold
    split = peers * wide
    for g in range(peers):
        for q, part in enumerate(parts):
            out_ref[g, q] = part[:, g * wide : (g + 1) * wide]
        lo = split + g * narrow
        out_ref[g, fold] = jnp.concatenate([part[:, lo : lo + narrow] for part in parts], axis=1)


def pack(rows, peers, wide, fold):
    depth, columns = rows.shape
    height = depth // fold
    tall = 32
    steps = height // tall

    def part(q):
        return pl.BlockSpec((tall, columns), lambda i: (q * steps + i, 0))

    out = call(
        pack_kernel, "pack",
        out_shape=jax.ShapeDtypeStruct((peers, fold + 1, height, wide), rows.dtype),
        grid=(steps,),
        in_specs=[part(q) for q in range(fold)],
        out_specs=pl.BlockSpec((peers, fold + 1, tall, wide), lambda i: (0, 0, i, 0)),
    )(*([in_hbm(rows)] * fold))
    return out.reshape(peers, depth + height, wide)


def squared(x):
    return jnp.square(x.astype(jnp.float32)).astype(jnp.bfloat16)


def square_kernel(states_ref, out_ref, sum_ref):
    turned = squared(states_ref[...].reshape(-1, states_ref.shape[3])).T
    out_ref[0] = turned
    part = jnp.sum(turned.astype(jnp.float32), axis=0, keepdims=True)

    @pl.when(pl.program_id(1) == 0)
    def _():
        sum_ref[0] = part

    @pl.when(pl.program_id(1) > 0)
    def _():
        sum_ref[0] += part


def squares(states, features, blocks):
    groups, ckpts, size, _ = states.shape
    tokens, tile = groups * size, features // blocks
    return call(
        square_kernel, "squares",
        out_shape=(
            jax.ShapeDtypeStruct((ckpts, features, tokens), jnp.bfloat16),
            jax.ShapeDtypeStruct((ckpts, 1, tokens), jnp.float32),
        ),
        grid=(ckpts, blocks),
        in_specs=[pl.BlockSpec((groups, 1, size, tile), lambda c, f: (0, c, 0, f))],
        out_specs=(
            pl.BlockSpec((1, tile, tokens), lambda c, f: (c, f, 0)),
            pl.BlockSpec((1, 1, tokens), lambda c, f: (c, 0, 0)),
        ),
    )(states)


def unfolded(block, fold):
    w = block.shape[1] // fold
    return jnp.concatenate([block[:, q * w : (q + 1) * w] for q in range(fold)], axis=0)


def padded(blocks, lanes):
    x = jnp.concatenate(blocks, axis=0)
    return jnp.concatenate([x, jnp.zeros((x.shape[0], lanes - x.shape[1]), x.dtype)], axis=1)


def score_kernel(states_ref, heads_ref, labels_ref, ids_ref, logits_ref, stats_ref):
    states = states_ref[...].reshape(-1, states_ref.shape[3])
    blocks, _, wide = heads_ref.shape[1:]
    depth = states.shape[1] // blocks
    slim = logits_ref.shape[2] - wide
    fold = wide // (slim // 2)
    narrow = padded([unfolded(heads_ref[0, b, depth:], fold) for b in range(blocks)], slim)
    heads = jnp.concatenate([heads_ref[0, b, :depth] for b in range(blocks)], axis=0)
    x = jnp.concatenate(
        [jnp.dot(states, y, preferred_element_type=jnp.float32) for y in (heads, narrow)], axis=1
    )
    x = jnp.where(ids_ref[...] >= 0, x, -3e38)
    logits_ref[0] = x
    top = jnp.max(x, axis=1, keepdims=True)
    grown = jnp.exp(x - top)
    target = labels_ref[...] == ids_ref[...]
    mass = jnp.sum(grown, axis=1, keepdims=True)
    hit = jnp.sum(jnp.where(target, grown, 0.0), axis=1, keepdims=True)
    square = jnp.sum(jnp.where(target, 0.0, grown * grown), axis=1, keepdims=True)
    lane = lax.broadcasted_iota(jnp.int32, (top.shape[0], 128), 1)
    table = jnp.where(lane == 0, top, jnp.where(lane == 1, mass, jnp.where(lane == 2, square, hit)))
    stats_ref[0] = table.T[:8]


def score(states, features, heads, labels, ids):
    groups, ckpts, size, _ = states.shape
    tokens, lanes = groups * size, ids.shape[1]
    return call(
        score_kernel, "score",
        out_shape=(
            pltpu.VMEM((ckpts, tokens, lanes), jnp.float32),
            jax.ShapeDtypeStruct((ckpts, 8, tokens), jnp.float32),
        ),
        grid=(ckpts,),
        in_specs=[
            pl.BlockSpec((groups, 1, size, features), lambda c: (0, c, 0, 0)),
            pl.BlockSpec((1, *heads.shape[1:]), lambda c: (c, 0, 0, 0)),
            pl.BlockSpec(labels.shape, lambda c: (0, 0)),
            pl.BlockSpec(ids.shape, lambda c: (0, 0)),
        ],
        out_specs=(
            pl.BlockSpec((1, tokens, lanes), lambda c: (c, 0, 0)),
            pl.BlockSpec((1, 8, tokens), lambda c: (c, 0, 0)),
        ),
    )(in_hbm(states), in_hbm(heads), labels, ids)


def merge_kernel(
    place_ref, scale_ref, logits_ref, table_ref, labels_ref, ids_ref, hidden_ref, heads_ref, *refs, prior
):
    outs, wide_rows, slim_rows, resid_ref = refs[:-3], *refs[-3:]
    ckpts, tokens, lanes = resid_ref.shape
    wide, depth = heads_ref.shape[3], hidden_ref.shape[1] // heads_ref.shape[0]
    first_row = pl.multiple_of((place_ref[0] ^ pl.program_id(0)) * depth, depth)
    slim = lanes - wide
    fold = wide // (slim // 2)

    @pl.when(pl.program_id(0) == 0)
    def _():
        target = jnp.where(labels_ref[...] == ids_ref[...], 1.0, 0.0)
        table = table_ref[...].T
        for c in range(ckpts):
            top, total = table[:, c : c + 1], table[:, ckpts + c : ckpts + c + 1]
            share = jnp.exp(logits_ref[c] - top) * (1.0 / total)
            resid_ref[c] = jnp.square(share - target).astype(jnp.bfloat16)

    def blend(lo, hi, heads_of):
        numer = denom = None
        for c in range(ckpts):
            product = jnp.dot(hidden_ref[c, pl.ds(first_row, depth)], resid_ref[c, :, lo:hi], preferred_element_type=jnp.float32)
            weight = (product * scale_ref[c] + prior).astype(jnp.bfloat16).astype(jnp.float32)
            term = weight * heads_of(c).astype(jnp.float32)
            numer = term if numer is None else numer + term
            denom = weight if denom is None else denom + weight
        return numer / denom

    wide_rows[...] = blend(0, wide, lambda c: heads_ref[c, 0, :depth])
    slim_rows[...] = blend(wide, lanes, lambda c: padded([unfolded(heads_ref[c, 0, depth:], fold)], slim))
    pair = outs[0].shape[0]
    halves = len(outs) // ckpts
    own = depth // (pair * halves)
    height = own // fold
    for plane in range(ckpts):

        @pl.when(pl.program_id(0) == plane)
        def _():
            for far in range(pair * halves):
                out_ref, slot = outs[plane * halves + far // pair], far % pair
                first = pl.multiple_of((place_ref[1] ^ far) * own, own)
                out_ref[slot, :own] = wide_rows[pl.ds(first, own)].astype(out_ref.dtype)
                rows = slim_rows[pl.ds(first, own)]
                block = jnp.concatenate(
                    [rows[q * height : (q + 1) * height, : slim // 2] for q in range(fold)], axis=1
                )
                rest = jnp.zeros((out_ref.shape[1] - own - height, wide), jnp.float32)
                out_ref[slot, own:] = jnp.concatenate([block, rest], axis=0).astype(out_ref.dtype)


def merge(place, scales, prior, logits, table, labels, ids, hidden_sq, heads, ntok):
    ckpts, blocks, _, width = heads.shape
    tokens, lanes = logits.shape[1:]
    depth = hidden_sq.shape[1] // blocks
    own = depth // ntok
    tall = own + -(-own * (lanes - width) // 2 // width // 16) * 16
    shape = (2, tall, width)

    def whole(x):
        return pl.BlockSpec(x.shape, lambda i, s: (0,) * x.ndim)

    return call(
        functools.partial(merge_kernel, prior=prior), "merge",
        out_shape=[jax.ShapeDtypeStruct(shape, jnp.bfloat16)] * (blocks * ntok // 2),
        grid_spec=pltpu.PrefetchScalarGridSpec(
            num_scalar_prefetch=1,
            grid=(blocks,),
            in_specs=[pl.BlockSpec(memory_space=pltpu.SMEM)]
            + [whole(x) for x in (logits, table, labels, ids)]
            + [
                pl.BlockSpec(memory_space=pltpu.VMEM),
                pl.BlockSpec((ckpts, 1, *heads.shape[2:]), lambda i, s: (0, s[0] ^ i, 0, 0)),
            ],
            out_specs=[pl.BlockSpec(shape, lambda i, s: (0, 0, 0))] * (blocks * ntok // 2),
            scratch_shapes=[
                pltpu.VMEM((depth, width), jnp.float32),
                pltpu.VMEM((depth, lanes - width), jnp.float32),
                pltpu.VMEM((ckpts, tokens, lanes), jnp.bfloat16),
            ],
        ),
    )(place, scales, pltpu.with_memory_space_constraint(logits, pltpu.VMEM), table, labels, ids, hidden_sq, in_hbm(heads))


def assemble_kernel(mine_ref, *refs, sources):
    arrays, out_ref = refs[:-1], refs[-1]
    own, columns = out_ref.shape
    wide = arrays[0].shape[2]
    narrow = columns // len(sources) - wide
    fold = wide // narrow
    height = own // fold
    mine = mine_ref[0]
    slim = []
    for r, (array, slot) in enumerate(sources):
        out_ref[:, pl.ds(pl.multiple_of((mine ^ r) * wide, wide), wide)] = arrays[array][slot, :own]
        slim.append(unfolded(arrays[array][slot, own:].astype(jnp.float32)[:height], fold))
    for r in range(0, len(sources), 2):
        ours, theirs = slim[r], slim[r + 1]
        odd = mine % 2 == 1
        pair = jnp.concatenate([jnp.where(odd, theirs, ours), jnp.where(odd, ours, theirs)], axis=1)
        first = len(sources) * wide + (mine ^ r) // 2 * 2 * narrow
        out_ref[:, pl.ds(pl.multiple_of(first, 2 * narrow), 2 * narrow)] = pair.astype(out_ref.dtype)


def assemble(mine, arrays, sources, own, columns):
    return call(
        functools.partial(assemble_kernel, sources=sources), "assemble",
        out_shape=jax.ShapeDtypeStruct((own, columns), jnp.bfloat16),
        in_specs=[pl.BlockSpec(memory_space=pltpu.SMEM)] + [pl.BlockSpec(memory_space=pltpu.VMEM)] * len(arrays),
        out_specs=pl.BlockSpec(memory_space=pltpu.VMEM),
    )(mine.astype(jnp.int32)[None], *arrays)


def after(value, *earlier):
    return lax.optimization_barrier((value, *earlier))[0] if earlier else value


def exchange(x):
    return lax.all_to_all(x, BOTH, 0, 0, tiled=True)


def combined(x, y):
    top = jnp.maximum(x[0], y[0])
    fx, fy = jnp.exp(x[0] - top), jnp.exp(y[0] - top)
    return jnp.stack(
        [top, x[1] * fx + y[1] * fy, x[2] * (fx * fx) + y[2] * (fy * fy), x[3] * fx + y[3] * fy]
    )


def everywhere(stats):
    for axis in ("tok", "vocab", "ckpt"):
        size, far = lax.axis_size(axis), 1
        while far < size:
            other = lax.ppermute(stats, axis, [(i, i ^ far) for i in range(size)])
            stats, far = combined(stats, other), far * 2
    return stats


def shards(heads, hidden, targets):
    ntok, nckpt, nvocab = (lax.axis_size(a) for a in ("tok", "ckpt", "vocab"))
    peers = nckpt * ntok
    mine = lax.axis_index("ckpt") * ntok + lax.axis_index("tok")
    rows = heads[0]
    depth, columns = rows.shape
    share = columns // peers
    wide = share // 128 * 128
    narrow = share - wide
    split = peers * wide
    per_device, features = hidden.shape[1:]
    tokens = per_device * ntok
    ckpts = nckpt
    fold = 4

    size = per_device // nvocab
    own = lax.dynamic_slice_in_dim(hidden[0], lax.axis_index("vocab") * size, size, 0)
    label = lax.dynamic_slice_in_dim(targets, lax.axis_index("vocab") * size, size, 0)[:, None]
    digits = jnp.concatenate([label % 256, label // 256 % 256, label // 65536], axis=1)
    digits = jnp.pad(digits.astype(hidden.dtype), ((0, 0), (0, 125)))
    own = own[None]

    def other(x, axis, far):
        return lax.ppermute(x, axis, [(i, i ^ far) for i in range(lax.axis_size(axis))])

    def paired(x, y, axis, far):
        upper = lax.axis_index(axis) // far % 2 == 1
        return jnp.concatenate([jnp.where(upper, y, x), jnp.where(upper, x, y)])

    planes = [own] + [other(own, "ckpt", far) for far in (2, 3, 1)]
    packed = pack(rows, peers, wide, fold)
    columns_in = exchange(packed).reshape(ckpts, ntok, depth + depth // fold, wide)
    states = paired(
        paired(planes[0], planes[3], "ckpt", 1), paired(planes[1], planes[2], "ckpt", 1), "ckpt", 2
    )[None]
    digits = jnp.broadcast_to(digits, (1, ckpts, *digits.shape))
    states = after(jnp.concatenate([states, digits], axis=3), packed)
    chains = [states, other(states, "tok", 2)]
    for i in (0, 1):
        far = 1
        while far < nvocab:
            chains[i] = paired(chains[i], other(chains[i], "vocab", far), "vocab", far)
            far *= 2
    states = paired(*chains, "tok", 2)
    states = paired(states, other(states, "tok", 1), "tok", 1)
    labels = states[:, 0, :, features : features + 3].reshape(tokens, 3).astype(jnp.int32)
    labels = labels[:, :1] + 256 * labels[:, 1:2] + 65536 * labels[:, 2:]
    if size % 16:
        states = states.transpose(1, 0, 2, 3).reshape(1, ckpts, tokens, features + 128)

    base = lax.axis_index("vocab") * columns
    pad = jnp.full((narrow,), -1)
    ids = jnp.concatenate(
        [base + mine * wide + jnp.arange(wide), base + split + mine * narrow + jnp.arange(narrow), pad]
    ).astype(jnp.int32)[None]
    hidden_sq, hidden_rows = squares(states, features, ntok)
    logits, stats = score(after(states, hidden_rows), features, columns_in, labels, ids)
    top, total, off, hit = everywhere(stats[:, :4].transpose(1, 0, 2))
    resid_rows = off / (total * total) + jnp.square(hit / total - 1.0)
    vocab_total = columns * nvocab
    count = float(tokens * features * vocab_total)
    level = jnp.sum(hidden_rows[:, 0] * resid_rows, axis=1) / jnp.float32(count)
    ratio = vocab_total / tokens
    shrink = 2.0 ** -math.ceil(math.log2(max(ratio, 1.0)))
    scales = jnp.float32(ratio * shrink) / level
    table = jnp.concatenate([top, total])

    place = jnp.stack([lax.axis_index("ckpt"), lax.axis_index("tok")]).astype(jnp.int32)
    parts = merge(
        place, scales, prior_weight * shrink, logits, table, labels, ids, hidden_sq, columns_in, ntok
    )
    arrays, sources, seconds = [], {}, []
    for half in reversed(range(peers // 2)):
        r, part = 2 * half, parts[half]
        if r:
            part = lax.ppermute(part, BOTH, [(g, g ^ r) for g in range(peers)])
        sources[r] = (len(arrays), 0)
        arrays.append(part)
        seconds.append((r + 1, part))
        if half in (peers // 4, 0):
            handed = other(jnp.stack([x[1] for _, x in seconds]), "tok", 1)
            for slot, (s, _) in enumerate(seconds):
                sources[s] = (len(arrays), slot)
            arrays.append(handed)
            seconds = []
    return assemble(mine, arrays, [sources[r] for r in range(peers)], depth // ntok, columns)


def solution(mesh):
    placed = (P("ckpt", "tok", "vocab"), P("ckpt", "tok", None), P("tok"))
    return jax.shard_map(
        shards, mesh=mesh, in_specs=placed, out_specs=P(("ckpt", "tok"), "vocab"), check_vma=False
    )
```

```python
import functools
import math

import jax
import jax.numpy as jnp
from jax import lax
from jax.experimental import pallas as pl
from jax.experimental.pallas import tpu as pltpu
from jax.sharding import PartitionSpec as P

prior_weight = 0.05
VMEM = 30 * 1024 * 1024
BOTH = ("ckpt", "tok")


def call(kernel, name, vmem=VMEM, **options):
    return pl.pallas_call(
        kernel, name=name, compiler_params=pltpu.CompilerParams(vmem_limit_bytes=vmem), **options
    )


def in_hbm(x):
    return pltpu.with_memory_space_constraint(x, pltpu.HBM)


def pack_kernel(*refs):
    parts, out_ref = refs[:-1], refs[-1]
    peers, blocks, _, wide = out_ref.shape
    fold = len(parts)
    narrow = wide // fold
    split = peers * wide
    for g in range(peers):
        for q, part in enumerate(parts):
            out_ref[g, q] = part[:, g * wide : (g + 1) * wide]
        lo = split + g * narrow
        out_ref[g, fold] = jnp.concatenate([part[:, lo : lo + narrow] for part in parts], axis=1)


def pack(rows, peers, wide, fold):
    depth, columns = rows.shape
    height = depth // fold
    tall = 32
    steps = height // tall

    def part(q):
        return pl.BlockSpec((tall, columns), lambda i: (q * steps + i, 0))

    out = call(
        pack_kernel, "pack",
        out_shape=jax.ShapeDtypeStruct((peers, fold + 1, height, wide), rows.dtype),
        grid=(steps,),
        in_specs=[part(q) for q in range(fold)],
        out_specs=pl.BlockSpec((peers, fold + 1, tall, wide), lambda i: (0, 0, i, 0)),
    )(*([in_hbm(rows)] * fold))
    return out.reshape(peers, depth + height, wide)


def squared(x):
    return jnp.square(x.astype(jnp.float32)).astype(jnp.bfloat16)


def square_kernel(states_ref, out_ref, sum_ref):
    turned = squared(states_ref[...].reshape(-1, states_ref.shape[3])).T
    out_ref[0] = turned
    part = jnp.sum(turned.astype(jnp.float32), axis=0, keepdims=True)

    @pl.when(pl.program_id(1) == 0)
    def _():
        sum_ref[0] = part

    @pl.when(pl.program_id(1) > 0)
    def _():
        sum_ref[0] += part


def squares(states, features, blocks):
    groups, ckpts, size, _ = states.shape
    tokens, tile = groups * size, features // blocks
    return call(
        square_kernel, "squares",
        out_shape=(
            jax.ShapeDtypeStruct((ckpts, features, tokens), jnp.bfloat16),
            jax.ShapeDtypeStruct((ckpts, 1, tokens), jnp.float32),
        ),
        grid=(ckpts, blocks),
        in_specs=[pl.BlockSpec((groups, 1, size, tile), lambda c, f: (0, c, 0, f))],
        out_specs=(
            pl.BlockSpec((1, tile, tokens), lambda c, f: (c, f, 0)),
            pl.BlockSpec((1, 1, tokens), lambda c, f: (c, 0, 0)),
        ),
    )(states)


def unfolded(block, fold):
    w = block.shape[1] // fold
    return jnp.concatenate([block[:, q * w : (q + 1) * w] for q in range(fold)], axis=0)


def padded(blocks, lanes):
    x = jnp.concatenate(blocks, axis=0)
    return jnp.concatenate([x, jnp.zeros((x.shape[0], lanes - x.shape[1]), x.dtype)], axis=1)


def score_kernel(states_ref, heads_ref, labels_ref, ids_ref, logits_ref, stats_ref):
    states = states_ref[...].reshape(-1, states_ref.shape[3])
    blocks, _, wide = heads_ref.shape[1:]
    depth = states.shape[1] // blocks
    slim = logits_ref.shape[2] - wide
    fold = wide // (slim // 2)
    narrow = padded([unfolded(heads_ref[0, b, depth:], fold) for b in range(blocks)], slim)
    heads = jnp.concatenate([heads_ref[0, b, :depth] for b in range(blocks)], axis=0)
    x = jnp.concatenate(
        [jnp.dot(states, y, preferred_element_type=jnp.float32) for y in (heads, narrow)], axis=1
    )
    x = jnp.where(ids_ref[...] >= 0, x, -3e38)
    logits_ref[0] = x
    top = jnp.max(x, axis=1, keepdims=True)
    grown = jnp.exp(x - top)
    target = labels_ref[...] == ids_ref[...]
    mass = jnp.sum(grown, axis=1, keepdims=True)
    hit = jnp.sum(jnp.where(target, grown, 0.0), axis=1, keepdims=True)
    square = jnp.sum(jnp.where(target, 0.0, grown * grown), axis=1, keepdims=True)
    lane = lax.broadcasted_iota(jnp.int32, (top.shape[0], 128), 1)
    table = jnp.where(lane == 0, top, jnp.where(lane == 1, mass, jnp.where(lane == 2, square, hit)))
    stats_ref[0] = table.T[:8]


def score(states, features, heads, labels, ids):
    groups, ckpts, size, _ = states.shape
    tokens, lanes = groups * size, ids.shape[1]
    return call(
        score_kernel, "score",
        out_shape=(
            pltpu.VMEM((ckpts, tokens, lanes), jnp.float32),
            jax.ShapeDtypeStruct((ckpts, 8, tokens), jnp.float32),
        ),
        grid=(ckpts,),
        in_specs=[
            pl.BlockSpec((groups, 1, size, features), lambda c: (0, c, 0, 0)),
            pl.BlockSpec((1, *heads.shape[1:]), lambda c: (c, 0, 0, 0)),
            pl.BlockSpec(labels.shape, lambda c: (0, 0)),
            pl.BlockSpec(ids.shape, lambda c: (0, 0)),
        ],
        out_specs=(
            pl.BlockSpec((1, tokens, lanes), lambda c: (c, 0, 0)),
            pl.BlockSpec((1, 8, tokens), lambda c: (c, 0, 0)),
        ),
    )(in_hbm(states), in_hbm(heads), labels, ids)


def merge_kernel(
    place_ref, scale_ref, logits_ref, table_ref, labels_ref, ids_ref, hidden_ref, heads_ref, *refs, prior
):
    outs, wide_rows, slim_rows, resid_ref = refs[:-3], *refs[-3:]
    ckpts, tokens, lanes = resid_ref.shape
    wide, depth = heads_ref.shape[3], hidden_ref.shape[1] // heads_ref.shape[0]
    first_row = pl.multiple_of((place_ref[0] ^ pl.program_id(0)) * depth, depth)
    slim = lanes - wide
    fold = wide // (slim // 2)

    @pl.when(pl.program_id(0) == 0)
    def _():
        target = jnp.where(labels_ref[...] == ids_ref[...], 1.0, 0.0)
        table = table_ref[...].T
        for c in range(ckpts):
            top, total = table[:, c : c + 1], table[:, ckpts + c : ckpts + c + 1]
            share = jnp.exp(logits_ref[c] - top) * (1.0 / total)
            resid_ref[c] = jnp.square(share - target).astype(jnp.bfloat16)

    def blend(lo, hi, heads_of):
        numer = denom = None
        for c in range(ckpts):
            product = jnp.dot(hidden_ref[c, pl.ds(first_row, depth)], resid_ref[c, :, lo:hi], preferred_element_type=jnp.float32)
            weight = (product * scale_ref[c] + prior).astype(jnp.bfloat16).astype(jnp.float32)
            term = weight * heads_of(c).astype(jnp.float32)
            numer = term if numer is None else numer + term
            denom = weight if denom is None else denom + weight
        return numer / denom

    wide_rows[...] = blend(0, wide, lambda c: heads_ref[c, 0, :depth])
    slim_rows[...] = blend(wide, lanes, lambda c: padded([unfolded(heads_ref[c, 0, depth:], fold)], slim))
    pair = 2
    halves = len(outs) // ckpts
    own = depth // (pair * halves)
    height = own // fold
    for plane in range(ckpts):

        @pl.when(pl.program_id(0) == plane)
        def _():
            for half in range(halves):
                out_ref, folded = outs[plane * halves + half], []
                for slot in range(pair):
                    first = pl.multiple_of((place_ref[1] ^ (half * pair + slot)) * own, own)
                    out_ref[slot * own : (slot + 1) * own] = wide_rows[pl.ds(first, own)].astype(out_ref.dtype)
                    rows = slim_rows[pl.ds(first, own)]
                    folded.append(
                        jnp.concatenate(
                            [rows[q * height : (q + 1) * height, : slim // 2] for q in range(fold)], axis=1
                        )
                    )
                out_ref[pair * own :] = jnp.concatenate(folded, axis=0).astype(out_ref.dtype)


def merge(place, scales, prior, logits, table, labels, ids, hidden_sq, heads, ntok):
    ckpts, blocks, _, width = heads.shape
    tokens, lanes = logits.shape[1:]
    depth = hidden_sq.shape[1] // blocks
    own = depth // ntok
    shape = (2 * own + own * (lanes - width) // width, width)

    def whole(x):
        return pl.BlockSpec(x.shape, lambda i, s: (0,) * x.ndim)

    return call(
        functools.partial(merge_kernel, prior=prior), "merge",
        out_shape=[jax.ShapeDtypeStruct(shape, jnp.bfloat16)] * (blocks * ntok // 2),
        grid_spec=pltpu.PrefetchScalarGridSpec(
            num_scalar_prefetch=1,
            grid=(blocks,),
            in_specs=[pl.BlockSpec(memory_space=pltpu.SMEM)]
            + [whole(x) for x in (logits, table, labels, ids)]
            + [
                pl.BlockSpec(memory_space=pltpu.VMEM),
                pl.BlockSpec((ckpts, 1, *heads.shape[2:]), lambda i, s: (0, s[0] ^ i, 0, 0)),
            ],
            out_specs=[pl.BlockSpec(shape, lambda i, s: (0, 0))] * (blocks * ntok // 2),
            scratch_shapes=[
                pltpu.VMEM((depth, width), jnp.float32),
                pltpu.VMEM((depth, lanes - width), jnp.float32),
                pltpu.VMEM((ckpts, tokens, lanes), jnp.bfloat16),
            ],
        ),
    )(place, scales, pltpu.with_memory_space_constraint(logits, pltpu.VMEM), table, labels, ids, hidden_sq, in_hbm(heads))


def assemble_kernel(mine_ref, *refs, sources):
    arrays, out_ref = refs[:-1], refs[-1]
    own, columns = out_ref.shape
    wide = arrays[0].shape[-1]
    narrow = columns // len(sources) - wide
    fold = wide // narrow
    height = own // fold
    mine = mine_ref[0]
    slim = []
    for r, (array, slot) in enumerate(sources):
        ref = arrays[array]
        if slot is None:
            block, rest = ref[:own], ref[2 * own :]
        else:
            block, rest = ref[slot, :own], ref[slot, own:]
        out_ref[:, pl.ds(pl.multiple_of((mine ^ r) * wide, wide), wide)] = block
        slim.append(unfolded(rest.astype(jnp.float32)[:height], fold))
    for r in range(0, len(sources), 2):
        ours, theirs = slim[r], slim[r + 1]
        odd = mine % 2 == 1
        pair = jnp.concatenate([jnp.where(odd, theirs, ours), jnp.where(odd, ours, theirs)], axis=1)
        first = len(sources) * wide + (mine ^ r) // 2 * 2 * narrow
        out_ref[:, pl.ds(pl.multiple_of(first, 2 * narrow), 2 * narrow)] = pair.astype(out_ref.dtype)


def assemble(mine, arrays, sources, own, columns):
    return call(
        functools.partial(assemble_kernel, sources=sources), "assemble",
        out_shape=jax.ShapeDtypeStruct((own, columns), jnp.bfloat16),
        in_specs=[pl.BlockSpec(memory_space=pltpu.SMEM)] + [pl.BlockSpec(memory_space=pltpu.VMEM)] * len(arrays),
        out_specs=pl.BlockSpec(memory_space=pltpu.VMEM),
    )(mine.astype(jnp.int32)[None], *arrays)


def after(value, *earlier):
    return lax.optimization_barrier((value, *earlier))[0] if earlier else value


def exchange(x):
    return lax.all_to_all(x, BOTH, 0, 0, tiled=True)


def combined(x, y):
    top = jnp.maximum(x[0], y[0])
    fx, fy = jnp.exp(x[0] - top), jnp.exp(y[0] - top)
    return jnp.stack(
        [top, x[1] * fx + y[1] * fy, x[2] * (fx * fx) + y[2] * (fy * fy), x[3] * fx + y[3] * fy]
    )


def everywhere(stats):
    for axis in ("tok", "vocab", "ckpt"):
        size, far = lax.axis_size(axis), 1
        while far < size:
            other = lax.ppermute(stats, axis, [(i, i ^ far) for i in range(size)])
            stats, far = combined(stats, other), far * 2
    return stats


def shards(heads, hidden, targets):
    ntok, nckpt, nvocab = (lax.axis_size(a) for a in ("tok", "ckpt", "vocab"))
    peers = nckpt * ntok
    mine = lax.axis_index("ckpt") * ntok + lax.axis_index("tok")
    rows = heads[0]
    depth, columns = rows.shape
    share = columns // peers
    wide = share // 128 * 128
    narrow = share - wide
    split = peers * wide
    per_device, features = hidden.shape[1:]
    tokens = per_device * ntok
    ckpts = nckpt
    fold = 4

    size = per_device // nvocab
    own = lax.dynamic_slice_in_dim(hidden[0], lax.axis_index("vocab") * size, size, 0)
    label = lax.dynamic_slice_in_dim(targets, lax.axis_index("vocab") * size, size, 0)[:, None]
    digits = jnp.concatenate([label % 256, label // 256 % 256, label // 65536], axis=1)
    digits = jnp.pad(digits.astype(hidden.dtype), ((0, 0), (0, 125)))
    own = own[None]

    def other(x, axis, far):
        return lax.ppermute(x, axis, [(i, i ^ far) for i in range(lax.axis_size(axis))])

    def paired(x, y, axis, far):
        upper = lax.axis_index(axis) // far % 2 == 1
        return jnp.concatenate([jnp.where(upper, y, x), jnp.where(upper, x, y)])

    planes = [own] + [other(own, "ckpt", far) for far in (2, 3, 1)]
    packed = pack(rows, peers, wide, fold)
    columns_in = exchange(packed).reshape(ckpts, ntok, depth + depth // fold, wide)
    states = paired(
        paired(planes[0], planes[3], "ckpt", 1), paired(planes[1], planes[2], "ckpt", 1), "ckpt", 2
    )[None]
    digits = jnp.broadcast_to(digits, (1, ckpts, *digits.shape))
    states = after(jnp.concatenate([states, digits], axis=3), packed)
    chains = [states, other(states, "tok", 2)]
    for i in (0, 1):
        far = 1
        while far < nvocab:
            chains[i] = paired(chains[i], other(chains[i], "vocab", far), "vocab", far)
            far *= 2
    states = paired(*chains, "tok", 2)
    states = paired(states, other(states, "tok", 1), "tok", 1)
    labels = states[:, 0, :, features : features + 3].reshape(tokens, 3).astype(jnp.int32)
    labels = labels[:, :1] + 256 * labels[:, 1:2] + 65536 * labels[:, 2:]
    if size % 16:
        states = states.transpose(1, 0, 2, 3).reshape(1, ckpts, tokens, features + 128)

    base = lax.axis_index("vocab") * columns
    pad = jnp.full((narrow,), -1)
    ids = jnp.concatenate(
        [base + mine * wide + jnp.arange(wide), base + split + mine * narrow + jnp.arange(narrow), pad]
    ).astype(jnp.int32)[None]
    hidden_sq, hidden_rows = squares(states, features, ntok)
    logits, stats = score(after(states, hidden_rows), features, columns_in, labels, ids)
    top, total, off, hit = everywhere(stats[:, :4].transpose(1, 0, 2))
    resid_rows = off / (total * total) + jnp.square(hit / total - 1.0)
    vocab_total = columns * nvocab
    count = float(tokens * features * vocab_total)
    level = jnp.sum(hidden_rows[:, 0] * resid_rows, axis=1) / jnp.float32(count)
    ratio = vocab_total / tokens
    shrink = 2.0 ** -math.ceil(math.log2(max(ratio, 1.0)))
    scales = jnp.float32(ratio * shrink) / level
    table = jnp.concatenate([top, total])

    place = jnp.stack([lax.axis_index("ckpt"), lax.axis_index("tok")]).astype(jnp.int32)
    parts = merge(
        place, scales, prior_weight * shrink, logits, table, labels, ids, hidden_sq, columns_in, ntok
    )
    arrays, sources, seconds = [], {}, []
    for half in reversed(range(peers // 2)):
        r, part = 2 * half, parts[half]
        if r:
            part = lax.ppermute(part, BOTH, [(g, g ^ r) for g in range(peers)])
        sources[r] = (len(arrays), None)
        arrays.append(part)
        seconds.append((r + 1, part))
        if half in (peers // 4, 0):
            own_rows = depth // ntok
            height = own_rows // fold
            pad = jnp.zeros((-height % 16, wide), jnp.bfloat16)
            handed = other(
                jnp.stack(
                    [
                        jnp.concatenate([x[own_rows : 2 * own_rows], x[2 * own_rows + height :], pad])
                        for _, x in seconds
                    ]
                ),
                "tok", 1,
            )
            for slot, (s, _) in enumerate(seconds):
                sources[s] = (len(arrays), slot)
            arrays.append(handed)
            seconds = []
    return assemble(mine, arrays, [sources[r] for r in range(peers)], depth // ntok, columns)


def solution(mesh):
    placed = (P("ckpt", "tok", "vocab"), P("ckpt", "tok", None), P("tok"))
    return jax.shard_map(
        shards, mesh=mesh, in_specs=placed, out_specs=P(("ckpt", "tok"), "vocab"), check_vma=False
    )
```

```python
import functools
import math

import jax
import jax.numpy as jnp
from jax import lax
from jax.experimental import pallas as pl
from jax.experimental.pallas import tpu as pltpu
from jax.sharding import PartitionSpec as P

prior_weight = 0.05
VMEM = 30 * 1024 * 1024
BOTH = ("ckpt", "tok")


def call(kernel, name, vmem=VMEM, **options):
    return pl.pallas_call(
        kernel, name=name, compiler_params=pltpu.CompilerParams(vmem_limit_bytes=vmem), **options
    )


def in_hbm(x):
    return pltpu.with_memory_space_constraint(x, pltpu.HBM)


def pack_kernel(*refs):
    parts, out_ref = refs[:-1], refs[-1]
    peers, blocks, _, wide = out_ref.shape
    fold = len(parts)
    narrow = wide // fold
    split = peers * wide
    for g in range(peers):
        for q, part in enumerate(parts):
            out_ref[g, q] = part[:, g * wide : (g + 1) * wide]
        lo = split + g * narrow
        out_ref[g, fold] = jnp.concatenate([part[:, lo : lo + narrow] for part in parts], axis=1)


def pack(rows, peers, wide, fold):
    depth, columns = rows.shape
    height = depth // fold
    tall = 32
    steps = height // tall

    def part(q):
        return pl.BlockSpec((tall, columns), lambda i: (q * steps + i, 0))

    out = call(
        pack_kernel, "pack",
        out_shape=jax.ShapeDtypeStruct((peers, fold + 1, height, wide), rows.dtype),
        grid=(steps,),
        in_specs=[part(q) for q in range(fold)],
        out_specs=pl.BlockSpec((peers, fold + 1, tall, wide), lambda i: (0, 0, i, 0)),
    )(*([in_hbm(rows)] * fold))
    return out.reshape(peers, depth + height, wide)


def squared(x):
    return jnp.square(x.astype(jnp.float32)).astype(jnp.bfloat16)


def square_kernel(states_ref, out_ref, sum_ref):
    turned = squared(states_ref[...].reshape(-1, states_ref.shape[3])).T
    out_ref[0] = turned
    part = jnp.sum(turned.astype(jnp.float32), axis=0, keepdims=True)

    @pl.when(pl.program_id(1) == 0)
    def _():
        sum_ref[0] = part

    @pl.when(pl.program_id(1) > 0)
    def _():
        sum_ref[0] += part


def squares(states, features, blocks):
    groups, ckpts, size, _ = states.shape
    tokens, tile = groups * size, features // blocks
    return call(
        square_kernel, "squares",
        out_shape=(
            jax.ShapeDtypeStruct((ckpts, features, tokens), jnp.bfloat16),
            jax.ShapeDtypeStruct((ckpts, 1, tokens), jnp.float32),
        ),
        grid=(ckpts, blocks),
        in_specs=[pl.BlockSpec((groups, 1, size, tile), lambda c, f: (0, c, 0, f))],
        out_specs=(
            pl.BlockSpec((1, tile, tokens), lambda c, f: (c, f, 0)),
            pl.BlockSpec((1, 1, tokens), lambda c, f: (c, 0, 0)),
        ),
    )(states)


def unfolded(block, fold):
    w = block.shape[1] // fold
    return jnp.concatenate([block[:, q * w : (q + 1) * w] for q in range(fold)], axis=0)


def padded(blocks, lanes):
    x = jnp.concatenate(blocks, axis=0)
    return jnp.concatenate([x, jnp.zeros((x.shape[0], lanes - x.shape[1]), x.dtype)], axis=1)


def score_kernel(states_ref, heads_ref, labels_ref, ids_ref, logits_ref, stats_ref):
    states = states_ref[...].reshape(-1, states_ref.shape[3])
    blocks, _, wide = heads_ref.shape[1:]
    depth = states.shape[1] // blocks
    slim = logits_ref.shape[2] - wide
    fold = wide // (slim // 2)
    narrow = padded([unfolded(heads_ref[0, b, depth:], fold) for b in range(blocks)], slim)
    heads = jnp.concatenate([heads_ref[0, b, :depth] for b in range(blocks)], axis=0)
    x = jnp.concatenate(
        [jnp.dot(states, y, preferred_element_type=jnp.float32) for y in (heads, narrow)], axis=1
    )
    x = jnp.where(ids_ref[...] >= 0, x, -3e38)
    logits_ref[0] = x
    top = jnp.max(x, axis=1, keepdims=True)
    grown = jnp.exp(x - top)
    target = labels_ref[...] == ids_ref[...]
    mass = jnp.sum(grown, axis=1, keepdims=True)
    hit = jnp.sum(jnp.where(target, grown, 0.0), axis=1, keepdims=True)
    square = jnp.sum(jnp.where(target, 0.0, grown * grown), axis=1, keepdims=True)
    lane = lax.broadcasted_iota(jnp.int32, (top.shape[0], 128), 1)
    table = jnp.where(lane == 0, top, jnp.where(lane == 1, mass, jnp.where(lane == 2, square, hit)))
    stats_ref[0] = table.T[:8]


def score(states, features, heads, labels, ids):
    groups, ckpts, size, _ = states.shape
    tokens, lanes = groups * size, ids.shape[1]
    return call(
        score_kernel, "score",
        out_shape=(
            pltpu.VMEM((ckpts, tokens, lanes), jnp.float32),
            jax.ShapeDtypeStruct((ckpts, 8, tokens), jnp.float32),
        ),
        grid=(ckpts,),
        in_specs=[
            pl.BlockSpec((groups, 1, size, features), lambda c: (0, c, 0, 0)),
            pl.BlockSpec((1, *heads.shape[1:]), lambda c: (c, 0, 0, 0)),
            pl.BlockSpec(labels.shape, lambda c: (0, 0)),
            pl.BlockSpec(ids.shape, lambda c: (0, 0)),
        ],
        out_specs=(
            pl.BlockSpec((1, tokens, lanes), lambda c: (c, 0, 0)),
            pl.BlockSpec((1, 8, tokens), lambda c: (c, 0, 0)),
        ),
    )(in_hbm(states), in_hbm(heads), labels, ids)


def merge_kernel(
    place_ref, scale_ref, logits_ref, table_ref, labels_ref, ids_ref, hidden_ref, heads_ref, *refs, prior
):
    outs, wide_rows, slim_rows, resid_ref = refs[:-3], *refs[-3:]
    ckpts, tokens, lanes = resid_ref.shape
    wide, depth = heads_ref.shape[3], hidden_ref.shape[1] // heads_ref.shape[0]
    first_row = pl.multiple_of((place_ref[0] ^ pl.program_id(0)) * depth, depth)
    slim = lanes - wide
    fold = wide // (slim // 2)

    @pl.when(pl.program_id(0) == 0)
    def _():
        target = jnp.where(labels_ref[...] == ids_ref[...], 1.0, 0.0)
        table = table_ref[...].T
        for c in range(ckpts):
            top, total = table[:, c : c + 1], table[:, ckpts + c : ckpts + c + 1]
            share = jnp.exp(logits_ref[c] - top) * (1.0 / total)
            resid_ref[c] = jnp.square(share - target).astype(jnp.bfloat16)

    def blend(lo, hi, heads_of):
        numer = denom = None
        for c in range(ckpts):
            product = jnp.dot(hidden_ref[c, pl.ds(first_row, depth)], resid_ref[c, :, lo:hi], preferred_element_type=jnp.float32)
            weight = (product * scale_ref[c] + prior).astype(jnp.bfloat16).astype(jnp.float32)
            term = weight * heads_of(c).astype(jnp.float32)
            numer = term if numer is None else numer + term
            denom = weight if denom is None else denom + weight
        return numer / denom

    wide_rows[...] = blend(0, wide, lambda c: heads_ref[c, 0, :depth])
    slim_rows[...] = blend(wide, lanes, lambda c: padded([unfolded(heads_ref[c, 0, depth:], fold)], slim))
    pair = 2
    halves = len(outs) // ckpts
    own = depth // (pair * halves)
    height = own // fold
    for plane in range(ckpts):

        @pl.when(pl.program_id(0) == plane)
        def _():
            for half in range(halves):
                out_ref, folded = outs[plane * halves + half], []
                for slot in range(pair):
                    first = pl.multiple_of((place_ref[1] ^ (half * pair + slot)) * own, own)
                    out_ref[slot * own : (slot + 1) * own] = wide_rows[pl.ds(first, own)].astype(out_ref.dtype)
                    rows = slim_rows[pl.ds(first, own)]
                    folded.append(
                        jnp.concatenate(
                            [rows[q * height : (q + 1) * height, : slim // 2] for q in range(fold)], axis=1
                        )
                    )
                out_ref[pair * own :] = jnp.concatenate(folded, axis=0).astype(out_ref.dtype)


def merge(place, scales, prior, logits, table, labels, ids, hidden_sq, heads, ntok):
    ckpts, blocks, _, width = heads.shape
    tokens, lanes = logits.shape[1:]
    depth = hidden_sq.shape[1] // blocks
    own = depth // ntok
    shape = (2 * own + own * (lanes - width) // width, width)

    def whole(x):
        return pl.BlockSpec(x.shape, lambda i, s: (0,) * x.ndim)

    return call(
        functools.partial(merge_kernel, prior=prior), "merge",
        out_shape=[jax.ShapeDtypeStruct(shape, jnp.bfloat16)] * (blocks * ntok // 2),
        grid_spec=pltpu.PrefetchScalarGridSpec(
            num_scalar_prefetch=1,
            grid=(blocks,),
            in_specs=[pl.BlockSpec(memory_space=pltpu.SMEM)]
            + [whole(x) for x in (logits, table, labels, ids)]
            + [
                pl.BlockSpec(memory_space=pltpu.VMEM),
                pl.BlockSpec((ckpts, 1, *heads.shape[2:]), lambda i, s: (0, s[0] ^ i, 0, 0)),
            ],
            out_specs=[pl.BlockSpec(shape, lambda i, s: (0, 0))] * (blocks * ntok // 2),
            scratch_shapes=[
                pltpu.VMEM((depth, width), jnp.float32),
                pltpu.VMEM((depth, lanes - width), jnp.float32),
                pltpu.VMEM((ckpts, tokens, lanes), jnp.bfloat16),
            ],
        ),
    )(place, scales, pltpu.with_memory_space_constraint(logits, pltpu.VMEM), table, labels, ids, hidden_sq, in_hbm(heads))


def assemble_kernel(mine_ref, *refs, sources):
    arrays, out_ref = refs[:-1], refs[-1]
    own, columns = out_ref.shape
    wide = arrays[0].shape[-1]
    narrow = columns // len(sources) - wide
    fold = wide // narrow
    height = own // fold
    mine = mine_ref[0]
    slim = []
    for r, (array, slot) in enumerate(sources):
        ref = arrays[array]
        if slot is None:
            block, rest = ref[:own], ref[2 * own :]
        else:
            block, rest = ref[slot, :own], ref[slot, own:]
        out_ref[:, pl.ds(pl.multiple_of((mine ^ r) * wide, wide), wide)] = block
        slim.append(unfolded(rest.astype(jnp.float32)[:height], fold))
    for r in range(0, len(sources), 2):
        ours, theirs = slim[r], slim[r + 1]
        odd = mine % 2 == 1
        pair = jnp.concatenate([jnp.where(odd, theirs, ours), jnp.where(odd, ours, theirs)], axis=1)
        first = len(sources) * wide + (mine ^ r) // 2 * 2 * narrow
        out_ref[:, pl.ds(pl.multiple_of(first, 2 * narrow), 2 * narrow)] = pair.astype(out_ref.dtype)


def assemble(mine, arrays, sources, own, columns):
    return call(
        functools.partial(assemble_kernel, sources=sources), "assemble",
        out_shape=jax.ShapeDtypeStruct((own, columns), jnp.bfloat16),
        in_specs=[pl.BlockSpec(memory_space=pltpu.SMEM)] + [pl.BlockSpec(memory_space=pltpu.VMEM)] * len(arrays),
        out_specs=pl.BlockSpec(memory_space=pltpu.VMEM),
    )(mine.astype(jnp.int32)[None], *arrays)


def after(value, *earlier):
    return lax.optimization_barrier((value, *earlier))[0] if earlier else value


def exchange(x):
    return lax.all_to_all(x, BOTH, 0, 0, tiled=True)


def combined(x, y):
    top = jnp.maximum(x[0], y[0])
    fx, fy = jnp.exp(x[0] - top), jnp.exp(y[0] - top)
    return jnp.stack(
        [top, x[1] * fx + y[1] * fy, x[2] * (fx * fx) + y[2] * (fy * fy), x[3] * fx + y[3] * fy]
    )


def everywhere(stats):
    for axis in ("tok", "ckpt", "vocab"):
        size, far = lax.axis_size(axis), 1
        while far < size:
            other = lax.ppermute(stats, axis, [(i, i ^ far) for i in range(size)])
            stats, far = combined(stats, other), far * 2
    return stats


def shards(heads, hidden, targets):
    ntok, nckpt, nvocab = (lax.axis_size(a) for a in ("tok", "ckpt", "vocab"))
    peers = nckpt * ntok
    mine = lax.axis_index("ckpt") * ntok + lax.axis_index("tok")
    rows = heads[0]
    depth, columns = rows.shape
    share = columns // peers
    wide = share // 128 * 128
    narrow = share - wide
    split = peers * wide
    per_device, features = hidden.shape[1:]
    tokens = per_device * ntok
    ckpts = nckpt
    fold = 4

    size = per_device // nvocab
    own = lax.dynamic_slice_in_dim(hidden[0], lax.axis_index("vocab") * size, size, 0)
    label = lax.dynamic_slice_in_dim(targets, lax.axis_index("vocab") * size, size, 0)[:, None]
    digits = jnp.concatenate([label % 256, label // 256 % 256, label // 65536], axis=1)
    digits = jnp.pad(digits.astype(hidden.dtype), ((0, 0), (0, 125)))
    own = own[None]

    def other(x, axis, far):
        return lax.ppermute(x, axis, [(i, i ^ far) for i in range(lax.axis_size(axis))])

    def paired(x, y, axis, far):
        upper = lax.axis_index(axis) // far % 2 == 1
        return jnp.concatenate([jnp.where(upper, y, x), jnp.where(upper, x, y)])

    planes = [own] + [other(own, "ckpt", far) for far in (2, 3, 1)]
    packed = pack(rows, peers, wide, fold)
    columns_in = exchange(packed).reshape(ckpts, ntok, depth + depth // fold, wide)
    states = paired(
        paired(planes[0], planes[3], "ckpt", 1), paired(planes[1], planes[2], "ckpt", 1), "ckpt", 2
    )[None]
    digits = jnp.broadcast_to(digits, (1, ckpts, *digits.shape))
    states = after(jnp.concatenate([states, digits], axis=3), packed)
    chains = [states, other(states, "tok", 2)]
    for i in (0, 1):
        far = 1
        while far < nvocab:
            chains[i] = paired(chains[i], other(chains[i], "vocab", far), "vocab", far)
            far *= 2
    states = paired(*chains, "tok", 2)
    states = paired(states, other(states, "tok", 1), "tok", 1)
    labels = states[:, 0, :, features : features + 3].reshape(tokens, 3).astype(jnp.int32)
    labels = labels[:, :1] + 256 * labels[:, 1:2] + 65536 * labels[:, 2:]
    if size % 16:
        states = states.transpose(1, 0, 2, 3).reshape(1, ckpts, tokens, features + 128)

    base = lax.axis_index("vocab") * columns
    pad = jnp.full((narrow,), -1)
    ids = jnp.concatenate(
        [base + mine * wide + jnp.arange(wide), base + split + mine * narrow + jnp.arange(narrow), pad]
    ).astype(jnp.int32)[None]
    hidden_sq, hidden_rows = squares(states, features, ntok)
    logits, stats = score(after(states, hidden_rows), features, columns_in, labels, ids)
    top, total, off, hit = everywhere(stats[:, :4].transpose(1, 0, 2))
    resid_rows = off / (total * total) + jnp.square(hit / total - 1.0)
    vocab_total = columns * nvocab
    count = float(tokens * features * vocab_total)
    level = jnp.sum(hidden_rows[:, 0] * resid_rows, axis=1) / jnp.float32(count)
    ratio = vocab_total / tokens
    shrink = 2.0 ** -math.ceil(math.log2(max(ratio, 1.0)))
    scales = jnp.float32(ratio * shrink) / level
    table = jnp.concatenate([top, total])

    place = jnp.stack([lax.axis_index("ckpt"), lax.axis_index("tok")]).astype(jnp.int32)
    parts = merge(
        place, scales, prior_weight * shrink, logits, table, labels, ids, hidden_sq, columns_in, ntok
    )
    arrays, sources, seconds = [], {}, []
    for half in reversed(range(peers // 2)):
        r, part = 2 * half, parts[half]
        if r:
            part = lax.ppermute(part, BOTH, [(g, g ^ r) for g in range(peers)])
        sources[r] = (len(arrays), None)
        arrays.append(part)
        seconds.append((r + 1, part))
        if half in (peers // 4, 0):
            own_rows = depth // ntok
            height = own_rows // fold
            pad = jnp.zeros((-height % 16, wide), jnp.bfloat16)
            handed = other(
                jnp.stack(
                    [
                        jnp.concatenate([x[own_rows : 2 * own_rows], x[2 * own_rows + height :], pad])
                        for _, x in seconds
                    ]
                ),
                "tok", 1,
            )
            for slot, (s, _) in enumerate(seconds):
                sources[s] = (len(arrays), slot)
            arrays.append(handed)
            seconds = []
    return assemble(mine, arrays, [sources[r] for r in range(peers)], depth // ntok, columns)


def solution(mesh):
    placed = (P("ckpt", "tok", "vocab"), P("ckpt", "tok", None), P("tok"))
    return jax.shard_map(
        shards, mesh=mesh, in_specs=placed, out_specs=P(("ckpt", "tok"), "vocab"), check_vma=False
    )
```
